512 devices in a mesh: attn: 32 (over x, z_lo, core), grp: 2 (over z_hi), tp: 8 (over y).
Axes of the slice: x: 4, y: 8, z: 8 (z_hi: 2, z_lo: 4; z = z_hi * 4 + z_lo), core: 2. Of those that a mesh axis runs over, the one named last changes fastest.
Arguments:
- queries: bfloat16 [1536, 6144], P(('attn', 'grp'), 'tp'), may hold values from -33 to 33
- new_keys: bfloat16 [1536, 1024], P(('attn', 'grp'), 'tp'), may hold values from -6 to 6
- new_values: bfloat16 [1536, 1024], P(('attn', 'grp'), 'tp'), may hold values from -6 to 6
- key_pages: bfloat16 [15360, 16, 1024], P(('attn', 'grp'), None, 'tp'), may hold values from -13 to 13
- value_pages: bfloat16 [15360, 16, 1024], P(('attn', 'grp'), None, 'tp'), may hold values from -6 to 6
- page_order: int32 [64, 240], P(('attn', 'grp')), may hold values from 0 to 239, each once within a row
- page_counts: int32 [64, 24], P(('attn', 'grp')), may hold values from 1 to 32, 240 in all within a row
- residual: bfloat16 [1536, 6144], P(('attn', 'grp'), 'tp'), may hold values from -3 to 3
- norm_gain: float32 [6144], P('tp'), may hold values from 0.1 to 1.9
- routes: int32 [1536, 2], P(('attn', 'grp')), may hold values from 0 to 7, all different within a row; in each aligned block of 24 rows (0 to 23, 24 to 47, ...) at most 12 rows name the same one
- route_weights: float32 [1536, 2], P(('attn', 'grp')), may hold values from 0.1 to 0.9
- w_gate: bfloat16 [2, 6144, 16384], P('grp', 'tp', 'attn'), may hold values from -0.078125 to 0.078125
- w_up: bfloat16 [2, 6144, 16384], P('grp', 'tp', 'attn'), may hold values from -0.078125 to 0.078125
- w_down: bfloat16 [2, 16384, 6144], P('grp', 'attn', 'tp'), may hold values from -0.046875 to 0.046875
Outputs:
- layer_out: bfloat16 [1536, 6144], P(('attn', 'grp'), 'tp')
The draws below stay inside these ranges and needn't reach their ends.
Inputs may be any that keep to these rules, and one draw needn't show every extreme that they name: `routes`: within one block of 24 rows the two experts of a row differ, and no expert is named by more than 12 rows of the block. Each row's page_order is a permutation of 0 to 239. `page_counts`: each block's counts sum to 240.
All inputs are finite; a program needn't handle non-finite values.
Results may differ from the reference program's by a relative error of at most 0.015.
Values may be sent and summed in bfloat16 or wider, within the bound.
A program may use at most 64 MiB of HBM per device.

```python
import math
import jax
import jax.numpy as jnp
import numpy as np
from jax import lax

D = 6144
HEADS = 48
KV = 8
HD = 128
FF = 16384
EXPERTS_ALL = 8
PAGE = 16
MAXP = 32
ROWS_DEV = 24
CAP = 12
POOL_PAGES = 240
ROWS = 1536
PAGES_ALL = 15360
N_ATTN = 32
N_GRP = 2
N_TP = 8


def draw_queries(key, part):
    key = jax.random.fold_in(key, 11)
    first = jax.random.fold_in(key, 0)
    values = jnp.clip(jax.random.normal(first, (ROWS, HEADS * HD), jnp.float32), -6.0, 6.0)
    return values.astype(jnp.bfloat16)


def draw_key_pages(key, part):
    key = jax.random.fold_in(key, 23)
    first = jax.random.fold_in(key, 0)
    values = jnp.clip(jax.random.normal(first, (PAGES_ALL, PAGE, KV * HD), jnp.float32), -6.0, 6.0)
    return values.astype(jnp.bfloat16)


def block_scale(rng, extent, cuts, smallest, high):
    gain, own = 1.0, jax.random.fold_in(rng, 6)
    for dim, shards_of in cuts:
        draws = jnp.exp(jax.random.uniform(jax.random.fold_in(own, dim), (shards_of,), jnp.float32, smallest / len(cuts), high / len(cuts)))
        gain = gain * jnp.repeat(draws, extent[dim] // shards_of).reshape([-1 if axis == dim else 1 for axis in range(len(extent))])
    return gain


def profile(number_of, total, limit, skew):
    portions = [(1 << 20) // math.isqrt(standing ** skew) + 1 for standing in range(2, number_of + 1)]
    rest, given = total - limit - (number_of - 1), [1] * (number_of - 1)
    while rest > 0:
        free = [i for i in range(number_of - 1) if given[i] < limit]
        pool, remaining = sum([portions[i] for i in free]), rest
        for i in free:
            addition = min(limit - given[i], max(1, remaining * portions[i] // pool), rest)
            given[i] = given[i] + addition
            rest = rest - addition
    return np.array([limit] + given)


def uneven(rng, number_of, total, bound, skew):
    if number_of == 2:
        one = jax.random.randint(rng, (), max(1, total - bound), min(bound, total - 1) + 1)
        return jnp.stack([one, total - one])
    lengths = jnp.asarray(profile(number_of, total, bound, skew), jnp.int32)
    couples = (number_of - 1) // 2
    source_of, sink = lengths[1:1 + 2 * couples:2], lengths[2:2 + 2 * couples:2]
    room = jnp.minimum(source_of - 1, bound - sink)
    passed = jax.random.randint(jax.random.fold_in(rng, 1), (couples,), 0, 1 << 20) % (room + 1)
    lengths = lengths.at[1:1 + 2 * couples:2].set(source_of - passed).at[2:2 + 2 * couples:2].set(sink + passed)
    return lengths[jax.random.permutation(jax.random.fold_in(rng, 2), number_of)]


def shared_out(key, own, number, rows, count, top, limit, slope):
    order = jax.random.permutation(key, count)
    packed, common = shares(count, rows * top, limit, slope, True), shares(count, rows * top, limit, slope, False)
    places = jnp.arange(count)

    def named(sizes, rotation):
        used = int((sizes > 0).sum())
        fixed = max(1, used // 4)
        passed = fixed + (places - fixed + rotation * (used - fixed)) % max(1, count - fixed)
        return jnp.zeros((count,), jnp.int32).at[order[jnp.where(places < fixed, places, passed)]].set(jnp.asarray(sizes, jnp.int32))

    sizes = jnp.where(number % 4 == 0, named(packed, number // 4), named(common, number - number // 4 - 1))
    mixed = jax.random.permutation(jax.random.fold_in(own, 3), count)
    source_of, taker = mixed[0:count // 2 * 2:2], mixed[1:count // 2 * 2:2]
    slack = jnp.minimum(sizes[source_of] - 1, limit - sizes[taker]) // 2
    slack = jnp.where((source_of == order[0]) | (taker == order[0]) | (sizes[taker] == 0), 0, jnp.maximum(slack, 0))
    passed = jax.random.randint(jax.random.fold_in(own, 4), (count // 2,), 0, 1 << 20) % (slack + 1)
    sizes = sizes.at[source_of].add(-passed).at[taker].add(passed)
    members = jnp.searchsorted(jnp.cumsum(sizes), jnp.arange(rows * top), side="right").astype(jnp.int32)
    grid = members.reshape(top, rows).T
    grid = grid[jax.random.permutation(jax.random.fold_in(own, 1), rows)]
    rotation = jax.random.randint(jax.random.fold_in(own, 2), (rows, 1), 0, top)
    return jnp.take_along_axis(grid, (jnp.arange(top)[None, :] + rotation) % top, axis=1)


def shares(amount, total, limit, lean, full):
    loads = [(1 << 20) // math.isqrt(rank ** lean) + 1 for rank in range(1, amount + 1)]
    largest = limit if full else min(limit, max(-(-total // amount), total * loads[0] // sum(loads)))
    least = 1 if total - largest >= amount - 1 else 0
    given, rest = [largest] + [least] * (amount - 1), total - largest - least * (amount - 1)
    while rest > 0:
        candidates = [i for i in range(1, amount) if given[i] < largest] or [i for i in range(1, amount) if given[i] < limit]
        mass, remaining = sum([loads[i] for i in candidates]), rest
        for i in candidates:
            addition = min(limit - given[i], max(1, remaining * loads[i] // mass), rest)
            given[i] = given[i] + addition
            rest = rest - addition
    return np.array(given)


def centred(stream_key, shape, spread, most, pieces=(), held_as=jnp.bfloat16):
    values = spread * jax.random.normal(stream_key, shape, jnp.float32)
    if pieces:
        values = values * block_scale(stream_key, shape, pieces, -0.22, 0.18)
    return jnp.clip(values, -most, most).astype(held_as)


def setup_inputs(seed: int = 0) -> dict:
    arg_keys = jax.random.split(jax.random.key(seed), 15)
    queries = draw_queries(jax.random.fold_in(arg_keys[14], 71), 0)
    new_keys = centred(arg_keys[1], (ROWS, KV * HD), 1.0, 6.0, ((0, 64), (1, 8)))
    new_values = centred(arg_keys[2], (ROWS, KV * HD), 1.0, 6.0, ((0, 64), (1, 8)))
    key_pages = draw_key_pages(jax.random.fold_in(arg_keys[14], 71), 0)
    value_pages = centred(arg_keys[4], (PAGES_ALL, PAGE, KV * HD), 1.0, 6.0, ((0, 64), (2, 8)))
    page_order = jax.vmap(lambda own: jax.random.permutation(own, POOL_PAGES))(jax.random.split(arg_keys[5], (N_ATTN * N_GRP))).reshape((N_ATTN * N_GRP, POOL_PAGES)).astype(jnp.int32)
    page_counts = jax.vmap(lambda own: uneven(own, ROWS_DEV, POOL_PAGES, MAXP, 2))(jax.random.split(arg_keys[6], (N_ATTN * N_GRP))).reshape((N_ATTN * N_GRP, ROWS_DEV)).astype(jnp.int32)
    residual = centred(arg_keys[7], (ROWS, D), 0.5, 3.0, ((0, 64), (1, 8)))
    norm_gain = jnp.clip(1.0 + 0.18 * jax.random.normal(arg_keys[8], (D,), jnp.float32), 0.1, 1.9)
    routes_keys = jax.random.split(jax.random.fold_in(arg_keys[9], 1), ROWS // ROWS_DEV)
    routes_turns = jax.random.permutation(jax.random.fold_in(arg_keys[9], 3), ROWS // ROWS_DEV)
    routes = jax.vmap(lambda own, number: shared_out(jax.random.fold_in(arg_keys[9], 2), own, number, ROWS_DEV, EXPERTS_ALL, 2, CAP, 2))(routes_keys, routes_turns).reshape((ROWS, 2))
    route_weights = jnp.clip(0.1 + 0.79999997 * jax.random.uniform(arg_keys[10], (ROWS, 2), jnp.float32) ** block_scale(arg_keys[10], (ROWS, 2), ((0, 64),), -0.2, 0.2), 0.1, 0.9)
    w_gate = centred(arg_keys[11], (N_GRP, D, FF), D ** -0.5, 0.078125, ((0, 2), (1, 8), (2, 32)))
    w_up = centred(arg_keys[12], (N_GRP, D, FF), D ** -0.5, 0.078125, ((0, 2), (1, 8), (2, 32)))
    w_down = centred(arg_keys[13], (N_GRP, FF, D), FF ** -0.5, 0.046875, ((0, 2), (1, 32), (2, 8)))
    return {"queries": queries, "new_keys": new_keys, "new_values": new_values, "key_pages": key_pages, "value_pages": value_pages, "page_order": page_order, "page_counts": page_counts, "residual": residual, "norm_gain": norm_gain, "routes": routes, "route_weights": route_weights, "w_gate": w_gate, "w_up": w_up, "w_down": w_down}


norm_epsilon = 1e-05

def attend(query, new_key, new_value, key_pages, value_pages, order, counts):
    count_rows = query.shape[0]
    kv_heads = new_key.shape[1] // HD
    group = query.shape[1] // new_key.shape[1]
    query_four = query.astype(jnp.float32).reshape(count_rows, kv_heads, group, HD)
    starts = (jnp.cumsum(counts) - counts).astype(jnp.int32)
    offsets = starts[:, None] + jnp.arange(MAXP, dtype=jnp.int32)[None, :]
    offsets = jnp.minimum(offsets, order.shape[0] - 1).astype(jnp.int32)
    pages = order[offsets]
    live = jnp.arange(MAXP, dtype=jnp.int32)[None, :] < counts[:, None]
    live = jnp.repeat(live, PAGE, axis=1)
    keys = key_pages[pages].astype(jnp.float32).reshape(count_rows, MAXP * PAGE, kv_heads, HD)
    values = value_pages[pages].astype(jnp.float32).reshape(count_rows, MAXP * PAGE, kv_heads, HD)
    scale = 1.0 / math.sqrt(HD)
    scores = jnp.einsum('rkgd,rtkd->rkgt', query_four, keys) * scale
    scores = jnp.where(live[:, None, None, :], scores, -1e+30)
    own_key = new_key.astype(jnp.float32).reshape(count_rows, kv_heads, HD)
    own = jnp.einsum('rkgd,rkd->rkg', query_four, own_key) * scale
    top = jnp.maximum(lax.optimization_barrier(jnp.max(scores, axis=3)), own)
    weights = jnp.exp(scores - top[..., None])
    own_weight = jnp.exp(own - top)
    total = lax.optimization_barrier(jnp.sum(weights, axis=3)) + own_weight
    weights_low = lax.optimization_barrier(weights.astype(jnp.bfloat16)).astype(jnp.float32)
    own_low = lax.optimization_barrier(own_weight.astype(jnp.bfloat16)).astype(jnp.float32)
    own_value = new_value.astype(jnp.float32).reshape(count_rows, kv_heads, 1, HD)
    mixed = jnp.einsum('rkgt,rtkd->rkgd', weights_low, values) + own_low[..., None] * own_value
    return (mixed / total[..., None]).reshape(count_rows, kv_heads * group * HD)

def expert_block(slots_in, gate_full, up_full, down_full):
    count_slots = slots_in.shape[0]
    unit_block = FF // N_ATTN
    x_split = slots_in.astype(jnp.float32).reshape(count_slots, N_TP, D // N_TP)

    def one_block(carry, block_index):
        begin = block_index * unit_block
        gate_part = lax.dynamic_slice_in_dim(gate_full, begin, unit_block, 1).astype(jnp.float32)
        up_part = lax.dynamic_slice_in_dim(up_full, begin, unit_block, 1).astype(jnp.float32)
        gate_part = gate_part.reshape(N_TP, D // N_TP, unit_block)
        up_part = up_part.reshape(N_TP, D // N_TP, unit_block)
        gate_terms = jnp.einsum('snd,ndf->snf', x_split, gate_part)
        up_terms = jnp.einsum('snd,ndf->snf', x_split, up_part)
        gate_sum = lax.optimization_barrier(jnp.sum(lax.optimization_barrier(gate_terms.astype(jnp.bfloat16)).astype(jnp.float32), axis=1))
        up_sum = lax.optimization_barrier(jnp.sum(lax.optimization_barrier(up_terms.astype(jnp.bfloat16)).astype(jnp.float32), axis=1))
        active = (jax.nn.silu(gate_sum) * up_sum).astype(jnp.bfloat16)
        down_part = lax.dynamic_slice_in_dim(down_full, begin, unit_block, 0)
        term = jnp.dot(active, down_part, preferred_element_type=jnp.float32)
        term = lax.optimization_barrier(term.astype(jnp.bfloat16)).astype(jnp.float32)
        return (carry + term, None)
    start_carry = jnp.zeros((count_slots, D), jnp.float32)
    result, unused = lax.scan(one_block, start_carry, jnp.arange(N_ATTN, dtype=jnp.int32))
    return result.astype(jnp.bfloat16)

def reference(queries, new_keys, new_values, key_pages, value_pages, page_order, page_counts, residual, norm_gain, routes, route_weights, w_gate, w_up, w_down):
    blocks = N_ATTN * N_GRP
    cap = ROWS_DEV // 2

    def per_block(items):
        return attend(*items)
    attention = lax.map(per_block, (queries.reshape(blocks, ROWS_DEV, HEADS * HD), new_keys.reshape(blocks, ROWS_DEV, KV * HD), new_values.reshape(blocks, ROWS_DEV, KV * HD), key_pages.reshape(blocks, POOL_PAGES, PAGE, KV * HD), value_pages.reshape(blocks, POOL_PAGES, PAGE, KV * HD), page_order, page_counts))
    hidden = (residual.reshape(blocks, ROWS_DEV, D).astype(jnp.float32) + attention).astype(jnp.bfloat16)
    hidden_wide = hidden.astype(jnp.float32)
    squares = lax.optimization_barrier(jnp.sum(hidden_wide * hidden_wide, axis=2))
    normed = (hidden_wide * lax.rsqrt(squares / D + norm_epsilon)[..., None] * norm_gain).astype(jnp.bfloat16)
    route_blocks = routes.reshape(blocks, ROWS_DEV, 2)
    weight_blocks = route_weights.reshape(blocks, ROWS_DEV, 2)
    onehot = route_blocks[..., None] == jnp.arange(N_GRP, dtype=jnp.int32)
    hits = jnp.any(onehot, axis=2).astype(jnp.int32)
    gating = lax.optimization_barrier(jnp.sum(weight_blocks[..., None] * onehot.astype(jnp.float32), axis=2))
    position = jnp.cumsum(hits, axis=1) - hits
    chosen = (hits[..., None] == 1) & (position[..., None] == jnp.arange(cap, dtype=jnp.int32))
    chooser = jnp.transpose(chosen.astype(jnp.float32), (0, 2, 3, 1))
    slots = jnp.einsum('necr,nrd->necd', chooser, normed.astype(jnp.float32)).astype(jnp.bfloat16)
    outputs = []
    for expert in range(N_GRP):
        slots_in = slots[:, expert].reshape(blocks * cap, D)
        outputs.append(expert_block(slots_in, w_gate[expert], w_up[expert], w_down[expert]).reshape(blocks, cap, D))
    out_all = jnp.stack(outputs, axis=1).astype(jnp.float32)
    brought = jnp.einsum('necr,necd->nred', chooser, out_all)
    expert_sum = lax.optimization_barrier(jnp.sum(gating[..., None] * brought, axis=2))
    return (hidden_wide + expert_sum).astype(jnp.bfloat16).reshape(ROWS, D)
```

```python
import functools
import math

import jax
import jax.numpy as jnp
from jax import lax
from jax.experimental import pallas as pl
from jax.experimental.pallas import tpu as pltpu
from jax.sharding import PartitionSpec as P

HD = 128
PAGE = 16
CAP = 12
SLOT = 16
PADR = 32
NX = 4
NCORE = 2
NORM_EPSILON = 1e-05
MASKED = -1e30
MESH = pl.DeviceIdType.MESH
F32 = jnp.float32
BF16 = jnp.bfloat16


def iota(shape, dim):
    return lax.broadcasted_iota(jnp.int32, shape, dim)


def to_column(row, rows):
    n = row.shape[1]
    eye = iota((rows, n), 0) == iota((rows, n), 1)
    return jnp.sum(jnp.where(eye, row, jnp.zeros_like(row)), axis=1, keepdims=True)


def to_row(column, lanes):
    n = column.shape[0]
    eye = iota((n, lanes), 0) == iota((n, lanes), 1)
    return jnp.sum(jnp.where(eye, column, jnp.zeros_like(column)), axis=0, keepdims=True)


def before(column, lanes):
    n = column.shape[0]
    ahead = iota((n, lanes), 0) < iota((n, lanes), 1)
    return jnp.sum(jnp.where(ahead, column, jnp.zeros_like(column)), axis=0, keepdims=True)


def dot(a, b):
    return jnp.dot(a, b, preferred_element_type=F32)


def kernel(
    sizes,
    q_ref,
    nk_ref,
    nv_ref,
    order_ref,
    counts_ref,
    res_ref,
    gain_ref,
    routes_ref,
    rw_ref,
    k_hbm,
    v_hbm,
    wg_hbm,
    wu_hbm,
    wd_hbm,
    out_ref,
    kaug,
    vbuf,
    wg,
    wu,
    wd,
    scores,
    sq_own,
    sq_in,
    hid,
    outg,
    zin,
    xin,
    pre,
    rs_in,
    act,
    outp,
    core_in,
    ysum,
    half_in,
    full_in,
    zsend,
    zback,
    local_sems,
    send_sems,
    recv_sems,
):
    nattn, ngrp, nt, width_all = sizes
    rows, width = q_ref.shape
    heads = width // HD
    pool = order_ref.shape[1]
    nzl = nattn // (NX * NCORE)
    nz = nzl * ngrp
    hr = nz * CAP
    nb = nt // 2
    half = nt // 2
    hh = hr // 2

    a = lax.axis_index("attn")
    g = lax.axis_index("grp")
    t = lax.axis_index("tp")
    core = lax.rem(a, NCORE)
    zl = lax.rem(a // NCORE, nzl)
    x = a // (NCORE * nzl)
    z = g * nzl + zl

    def at_x(d):
        return {"attn": (lax.rem(x + d, NX) * nzl + zl) * NCORE + core, "grp": g, "tp": t}

    def at_z(d):
        to = lax.rem(z + d, nz)
        return {"attn": (x * nzl + lax.rem(to, nzl)) * NCORE + core, "grp": to // nzl, "tp": t}

    def at_t(d):
        return {"attn": a, "grp": g, "tp": lax.rem(t + d, nt)}

    sibling = {"attn": a + 1 - 2 * core, "grp": g, "tp": t}

    barrier = pltpu.get_barrier_semaphore()
    partners = [sibling, at_x(1), at_x(NX - 1)]
    partners += [at_z(d) for d in range(1, nz)]
    partners += [at_t(d) for d in range(1, nt)]
    for partner in partners:
        pl.semaphore_signal(barrier, inc=1, device_id=partner, device_id_type=MESH)

    loads = [
        pltpu.make_async_copy(k_hbm, kaug.at[:, :, pl.ds(0, HD)], local_sems.at[0]),
        pltpu.make_async_copy(v_hbm, vbuf, local_sems.at[1]),
        pltpu.make_async_copy(wg_hbm.at[0], wg, local_sems.at[2]),
        pltpu.make_async_copy(wu_hbm.at[0], wu, local_sems.at[3]),
        pltpu.make_async_copy(wd_hbm.at[0], wd, local_sems.at[4]),
    ]
    for load in loads:
        load.start()

    sent = []

    def push(src, dst, to):
        index = len(sent)
        copy = pltpu.make_async_remote_copy(
            src_ref=src,
            dst_ref=dst,
            send_sem=send_sems.at[index],
            recv_sem=recv_sems.at[index],
            device_id=to,
            device_id_type=MESH,
        )
        copy.start()
        sent.append(copy)
        return copy

    counts_col = to_column(counts_ref[...].astype(F32), rows)
    starts_row = before(counts_col, HD)
    counts_row = to_row(counts_col, HD)
    place = iota((pool, HD), 0).astype(F32)
    row_of_place = ((place >= starts_row) & (place < starts_row + counts_row)).astype(F32)
    place_of_page = (iota((pool, pool), 0) == order_ref[...]).astype(F32)
    owner = dot(place_of_page.astype(BF16), row_of_place.astype(BF16))
    kaug[:, :, pl.ds(HD, HD)] = jnp.broadcast_to(
        owner.reshape(pool, 1, HD), (pool, PAGE, HD)
    ).astype(BF16)
    own_row = iota((rows, HD), 0)
    lane = iota((rows, HD), 1)
    mask_block = jnp.where((own_row == lane) | (lane >= rows), 0.0, MASKED)

    q_wide = q_ref[...].astype(F32)
    q_rows = jnp.concatenate([q_wide[:, h * HD : (h + 1) * HD] for h in range(heads)], axis=0)
    q_aug = jnp.concatenate(
        [q_rows, jnp.concatenate([mask_block] * heads, axis=0)], axis=1
    ).astype(BF16)
    scale = 1.0 / math.sqrt(HD)
    new_key = jnp.concatenate([nk_ref[...].astype(F32)] * heads, axis=0)
    own = jnp.sum(q_rows * new_key, axis=1, keepdims=True) * scale

    loads[0].wait()
    pieces = scores.shape[0]
    pages = pool // pieces
    tokens = pages * PAGE

    def score_piece(i, top):
        keys = kaug[pl.ds(i * pages, pages)].reshape(tokens, 2 * HD)
        piece = (
            lax.dot_general(
                q_aug, keys, (((1,), (1,)), ((), ())), preferred_element_type=F32
            )
            * scale
        )
        scores[i] = piece
        return jnp.maximum(top, piece)

    top = lax.fori_loop(
        0, pieces, score_piece, jnp.full((heads * rows, tokens), MASKED, F32), unroll=True
    )
    top = jnp.maximum(jnp.max(top, axis=1, keepdims=True), own)
    own_weight = jnp.exp(own - top)

    loads[1].wait()

    def value_piece(i, carry):
        total, mixed = carry
        weights = jnp.exp(scores[i] - top)
        values = vbuf[pl.ds(i * pages, pages)].reshape(tokens, HD)
        return total + weights, mixed + dot(weights.astype(BF16), values)

    total, mixed = lax.fori_loop(
        0,
        pieces,
        value_piece,
        (jnp.zeros((heads * rows, tokens), F32), jnp.zeros((heads * rows, HD), F32)),
        unroll=True,
    )
    total = jnp.sum(total, axis=1, keepdims=True) + own_weight
    own_low = own_weight.astype(BF16).astype(F32)
    new_value = jnp.concatenate([nv_ref[...].astype(F32)] * heads, axis=0)
    attention = (mixed + own_low * new_value) / total
    attention = jnp.concatenate(
        [attention[h * rows : (h + 1) * rows] for h in range(heads)], axis=1
    )
    hidden = (res_ref[...].astype(F32) + attention).astype(BF16).astype(F32)
    hid[...] = hidden
    squares = jnp.sum(hidden * hidden, axis=1, keepdims=True)
    sq_own[...] = jnp.broadcast_to(to_row(squares, HD), sq_own.shape)

    routes = routes_ref[...]
    route_weights = rw_ref[...]
    chosen, gated = [], []
    for e in range(ngrp):
        named = routes == e
        hit_row = jnp.max(named.astype(F32), axis=0, keepdims=True)
        gate_row = jnp.sum(jnp.where(named, route_weights, 0.0), axis=0, keepdims=True)
        hit_col = to_column(hit_row, PADR)
        gate_col = to_column(gate_row, PADR)
        pos_row = before(hit_col, PADR)
        pos_col = to_column(pos_row, PADR)
        hit_wide = to_row(hit_col, PADR)
        slot = iota((SLOT, PADR), 0).astype(F32)
        chosen.append(jnp.where(slot == pos_row, hit_wide, 0.0))
        slot = iota((PADR, SLOT), 1).astype(F32)
        gated.append(jnp.where(slot == pos_col, hit_col * gate_col, 0.0))
    chooser = jnp.concatenate(chosen, axis=0).astype(BF16)
    gating = jnp.concatenate(gated, axis=1)

    pl.semaphore_wait(barrier, len(partners))

    copies = [push(sq_own, sq_in.at[d], at_t(d)) for d in range(1, nt)]
    for copy in copies:
        copy.wait_recv()
    total_row = sq_own[...]
    for d in range(1, nt):
        total_row = total_row + sq_in[d]
    squares = to_column(total_row[0:1, 0:rows], rows)
    normed = hid[...] * lax.rsqrt(squares / width_all + NORM_EPSILON) * gain_ref[...]
    normed = jnp.concatenate([normed, jnp.zeros((PADR - rows, width), F32)], axis=0)
    outgoing = dot(chooser, normed.astype(BF16)).astype(BF16)
    for e in range(ngrp):
        outg[e] = outgoing[e * SLOT : (e + 1) * SLOT]

    copies = [
        push(outg.at[lax.rem(z + d, nz) // nzl], zin.at[d], at_z(d)) for d in range(1, nz)
    ]
    zin[0] = outg[g]
    for copy in copies:
        copy.wait_recv()
    packed = iota((hr, nz * SLOT), 0)
    padded = iota((hr, nz * SLOT), 1)
    match = (packed // CAP == padded // SLOT) & (packed % CAP == padded % SLOT)
    pack = match.astype(F32).astype(BF16)
    xin[0, 0] = dot(pack, zin[...].reshape(nz * SLOT, width)).astype(BF16)

    core_copy = {0: push(xin.at[0, 0], xin.at[0, 1], sibling)}
    x_copy = {
        1: push(xin.at[0, 0], xin.at[1, 0], at_x(1)),
        3: push(xin.at[0, 0], xin.at[3, 0], at_x(3)),
    }
    relay = []
    low, high = pl.ds(0, hh), pl.ds(hh, hh)

    def task_x1():
        x_copy[1].wait_recv()
        relay.append(push(xin.at[1, 0, low], xin.at[2, 0, low], at_x(1)))
        core_copy[1] = push(xin.at[1, 0], xin.at[1, 1], sibling)
        x_copy[3].wait_recv()
        relay.append(push(xin.at[3, 0, high], xin.at[2, 0, high], at_x(3)))
        core_copy[3] = push(xin.at[3, 0], xin.at[3, 1], sibling)

    def task_x2():
        for copy in relay:
            copy.wait_recv()
        core_copy[2] = push(xin.at[2, 0], xin.at[2, 1], sibling)

    def block(o):
        return lax.rem(t + o + nt, nt)

    rs = {}

    def task_m1(c):
        if c == 0:
            loads[2].wait()
            loads[3].wait()
        core_copy[c].wait_recv()
        slots = xin[c].reshape(2 * hr, width)
        for part, weight in enumerate((wg, wu)):
            result = dot(slots, weight[...]).astype(BF16)
            for b in range(nb):
                for h in range(2):
                    pre[c, 2 * b + h, part] = result[
                        h * hr : (h + 1) * hr, b * HD : (b + 1) * HD
                    ]
        far = block(half)
        rs[c] = (
            push(pre.at[c, far, 0], rs_in.at[c, 0, 0, 0], at_t(1)),
            push(pre.at[c, far, 1], rs_in.at[c, 1, 0, 1], at_t(nt - 1)),
        )

    def task_rs(c, step):
        down = block(half - step)
        up = block(step - half)
        out = []
        for way, (copy, here, to) in enumerate(
            zip(rs[c], (down, up), (at_t(1), at_t(nt - 1)))
        ):
            copy.wait_recv()
            if step == 1:
                pre[c, here, way] = (
                    pre[c, here, way].astype(F32) + rs_in[c, way, 0, way].astype(F32)
                ).astype(BF16)
            else:
                pre[c, here] = (
                    pre[c, here].astype(F32) + rs_in[c, way, step - 1].astype(F32)
                ).astype(BF16)
            out.append(push(pre.at[c, here], rs_in.at[c, way, step], to))
        rs[c] = tuple(out)

    ag = {}

    def task_silu(c):
        for copy in rs[c]:
            copy.wait_recv()
        total = pre[c, t].astype(F32)
        if half > 1:
            total = total + rs_in[c, 0, half - 1].astype(F32)
            total = total + rs_in[c, 1, half - 1].astype(F32)
            gate, up = total[0], total[1]
        else:
            gate = total[0] + rs_in[c, 0, 0, 0].astype(F32)
            up = total[1] + rs_in[c, 1, 0, 1].astype(F32)
        act[c, t] = (gate / (1.0 + jnp.exp(-gate)) * up).astype(BF16)
        send_act(c, 0)

    def send_act(c, hop):
        right = act.at[c, block(-hop)]
        left = act.at[c, block(hop)]
        if hop == half - 1:
            right, left = right.at[low], left.at[high]
        ag[c] = (push(right, right, at_t(1)), push(left, left, at_t(nt - 1)))

    def task_ag(c, hop):
        for copy in ag[c]:
            copy.wait_recv()
        send_act(c, hop)

    def task_m2(c):
        if c == 0:
            loads[4].wait()
        for copy in ag[c]:
            copy.wait_recv()
        for h in (1, 0):
            units = jnp.concatenate([act[c, 2 * b + h] for b in range(nb)], axis=1)
            outp[c, h] = dot(units, wd[...]).astype(BF16)
            if h == 1:
                core_copy[c] = push(outp.at[c, 1], core_in.at[c], sibling)

    def task_core(c):
        core_copy[c].wait_recv()
        ysum[c] = (outp[c, 0].astype(F32) + core_in[c].astype(F32)).astype(BF16)
        if c == 2:
            halves.append(push(ysum.at[2, low], half_in.at[0], at_x(3)))
            halves.append(push(ysum.at[2, high], half_in.at[1], at_x(1)))

    halves = []
    x_back = []

    def task_x_back():
        for way, (c, part, to) in enumerate(((1, low, at_x(3)), (3, high, at_x(1)))):
            halves[way].wait_recv()
            ysum[c, part] = (ysum[c, part].astype(F32) + half_in[way].astype(F32)).astype(BF16)
            x_back.append(push(ysum.at[c], full_in.at[way], to))

    stages = [task_m1]
    stages += [functools.partial(task_rs, step=s) for s in range(1, half)]
    stages += [task_silu]
    stages += [functools.partial(task_ag, hop=h) for h in range(1, half)]
    stages += [task_m2, task_core]
    for k in range(len(stages) + 2 * (NX - 1)):
        for c in range(NX):
            if 0 <= k - 2 * c < len(stages):
                stages[k - 2 * c](c)
        if k == 1:
            task_x1()
        if k == 3:
            task_x2()
    task_x_back()
    for copy in x_back:
        copy.wait_recv()
    mine = (
        ysum[0].astype(F32) + full_in[0].astype(F32) + full_in[1].astype(F32)
    ).astype(BF16)
    spread = lax.dot_general(pack, mine, (((0,), (0,)), ((), ())), preferred_element_type=F32)
    zsend[...] = spread.astype(BF16).reshape(nz, SLOT, width)

    copies = [push(zsend.at[d], zback.at[d], at_z(nz - d)) for d in range(1, nz)]
    zback[0] = zsend[0]
    for copy in copies:
        copy.wait_recv()
    experts = [jnp.zeros((SLOT, width), F32) for e in range(ngrp)]
    for d in range(nz):
        expert = lax.rem(z + d, nz) // nzl
        piece = zback[d].astype(F32)
        for e in range(ngrp):
            experts[e] = experts[e] + piece * (expert == e).astype(F32)
    brought = jnp.concatenate(experts, axis=0).astype(BF16)
    gate_high = gating.astype(BF16)
    gate_low = (gating - gate_high.astype(F32)).astype(BF16)
    expert_sum = dot(gate_high, brought) + dot(gate_low, brought)
    out_ref[...] = (hid[...] + expert_sum[0:rows]).astype(BF16)

    for copy in sent:
        copy.wait_send()


def local(
    sizes,
    queries,
    new_keys,
    new_values,
    key_pages,
    value_pages,
    page_order,
    page_counts,
    residual,
    norm_gain,
    routes,
    route_weights,
    w_gate,
    w_up,
    w_down,
):
    nattn, ngrp, nt, width_all = sizes
    rows, width = queries.shape
    heads = width // HD
    pool = key_pages.shape[0]
    units = w_gate.shape[2]
    nzl = nattn // (NX * NCORE)
    nz = nzl * ngrp
    hr = nz * CAP
    half = nt // 2
    pieces = pool // 16
    copies = 200
    vmem = pl.BlockSpec(memory_space=pltpu.VMEM)
    hbm = pl.BlockSpec(memory_space=pl.ANY)
    return pl.pallas_call(
        functools.partial(kernel, sizes),
        out_shape=jax.ShapeDtypeStruct((rows, width), BF16),
        in_specs=[vmem] * 9 + [hbm] * 5,
        out_specs=vmem,
        scratch_shapes=[
            pltpu.VMEM((pool, PAGE, 2 * HD), BF16),
            pltpu.VMEM((pool, PAGE, HD), BF16),
            pltpu.VMEM((width, units), BF16),
            pltpu.VMEM((width, units), BF16),
            pltpu.VMEM((units, width), BF16),
            pltpu.VMEM((pieces, heads * rows, 16 * PAGE), F32),
            pltpu.VMEM((8, HD), F32),
            pltpu.VMEM((nt, 8, HD), F32),
            pltpu.VMEM((rows, width), F32),
            pltpu.VMEM((ngrp, SLOT, width), BF16),
            pltpu.VMEM((nz, SLOT, width), BF16),
            pltpu.VMEM((NX, 2, hr, width), BF16),
            pltpu.VMEM((NX, nt, 2, hr, HD), BF16),
            pltpu.VMEM((NX, 2, half, 2, hr, HD), BF16),
            pltpu.VMEM((NX, nt, hr, HD), BF16),
            pltpu.VMEM((NX, 2, hr, width), BF16),
            pltpu.VMEM((NX, hr, width), BF16),
            pltpu.VMEM((NX, hr, width), BF16),
            pltpu.VMEM((2, hr // 2, width), BF16),
            pltpu.VMEM((2, hr, width), BF16),
            pltpu.VMEM((nz, SLOT, width), BF16),
            pltpu.VMEM((nz, SLOT, width), BF16),
            pltpu.SemaphoreType.DMA((5,)),
            pltpu.SemaphoreType.DMA((copies,)),
            pltpu.SemaphoreType.DMA((copies,)),
        ],
        compiler_params=pltpu.CompilerParams(
            collective_id=0, has_side_effects=True, vmem_limit_bytes=48 * 1024 * 1024
        ),
    )(
        queries,
        new_keys,
        new_values,
        page_order,
        page_counts,
        residual,
        norm_gain.reshape(1, width),
        routes.T,
        route_weights.T,
        key_pages,
        value_pages,
        w_gate,
        w_up,
        w_down,
    )


def solution(mesh):
    sizes = (mesh.shape["attn"], mesh.shape["grp"], mesh.shape["tp"])

    def whole(*arrays):
        return jax.shard_map(
            functools.partial(local, sizes + (arrays[0].shape[1],)),
            mesh=mesh,
            in_specs=(
                P(("attn", "grp"), "tp"),
                P(("attn", "grp"), "tp"),
                P(("attn", "grp"), "tp"),
                P(("attn", "grp"), None, "tp"),
                P(("attn", "grp"), None, "tp"),
                P(("attn", "grp"), None),
                P(("attn", "grp"), None),
                P(("attn", "grp"), "tp"),
                P("tp"),
                P(("attn", "grp"), None),
                P(("attn", "grp"), None),
                P("grp", "tp", "attn"),
                P("grp", "tp", "attn"),
                P("grp", "attn", "tp"),
            ),
            out_specs=P(("attn", "grp"), "tp"),
            check_vma=False,
        )(*arrays)

    return whole
```

```python
import functools
import math

import jax
import jax.numpy as jnp
from jax import lax
from jax.experimental import pallas as pl
from jax.experimental.pallas import tpu as pltpu
from jax.sharding import PartitionSpec as P

HD = 128
PAGE = 16
CAP = 12
SLOT = 16
PADR = 32
NX = 4
NCORE = 2
NORM_EPSILON = 1e-05
MASKED = -1e30
MESH = pl.DeviceIdType.MESH
IN, M1, RS2, SILU, AG2, M2, HOME, BACK = range(8)
ORDER = (
    (IN, 0), (M1, 0), (IN, 7), (M1, 7), (IN, 2), (IN, 3), (RS2, 0), (IN, 1), (M1, 2), (IN, 5),
    (M1, 1), (M1, 3), (IN, 4), (M1, 5), (IN, 6), (M1, 6), (M1, 4), (RS2, 3), (RS2, 5),
    (RS2, 2), (RS2, 6), (RS2, 1), (SILU, 3), (RS2, 4), (SILU, 5), (SILU, 2), (SILU, 6),
    (RS2, 7), (AG2, 3), (SILU, 1), (SILU, 4), (SILU, 0), (AG2, 6), (AG2, 5), (AG2, 2),
    (SILU, 7), (M2, 3), (AG2, 1), (AG2, 4), (HOME, 3), (AG2, 0), (M2, 6), (M2, 5), (M2, 2),
    (HOME, 6), (AG2, 7), (HOME, 2), (M2, 1), (HOME, 5), (M2, 4), (HOME, 1), (M2, 0), (HOME, 4),
    (M2, 7), (BACK, 0), (BACK, 1),
)
F32 = jnp.float32
BF16 = jnp.bfloat16


def z_groups(nz):
    if nz == 2:
        return ((0,), (1,))
    quarter = nz // 4
    near = tuple(range(quarter + 1)) + tuple(range(nz - quarter + 1, nz))
    return near, tuple(d for d in range(nz) if d not in near)


def iota(shape, dim):
    return lax.broadcasted_iota(jnp.int32, shape, dim)


def to_column(row, rows, start=0):
    n = row.shape[1]
    eye = iota((rows, n), 0) + start == iota((rows, n), 1)
    return jnp.sum(jnp.where(eye, row, jnp.zeros_like(row)), axis=1, keepdims=True)


def to_row(column, lanes, start=0):
    n = column.shape[0]
    eye = iota((n, lanes), 0) + start == iota((n, lanes), 1)
    return jnp.sum(jnp.where(eye, column, jnp.zeros_like(column)), axis=0, keepdims=True)


def before(column, lanes):
    n = column.shape[0]
    ahead = iota((n, lanes), 0) < iota((n, lanes), 1)
    return jnp.sum(jnp.where(ahead, column, jnp.zeros_like(column)), axis=0, keepdims=True)


def dot(a, b):
    return jnp.dot(a, b, preferred_element_type=F32)


def kernel(
    sizes,
    q_hbm,
    nk_hbm,
    nv_hbm,
    order_hbm,
    counts_hbm,
    res_hbm,
    gain_hbm,
    routes_hbm,
    rw_hbm,
    k_hbm,
    v_hbm,
    wg_hbm,
    wu_hbm,
    wd_hbm,
    out_ref,
    q_ref,
    nk_ref,
    nv_ref,
    order_ref,
    counts_ref,
    res_ref,
    gain_ref,
    routes_ref,
    rw_ref,
    kaug,
    vbuf,
    wg,
    wu,
    wd,
    scores,
    sq_own,
    sq_in,
    hid,
    outg,
    zin,
    xin,
    pre,
    rs_half,
    rs_in,
    act,
    outp,
    core_in,
    xsend,
    xback,
    zsend,
    zback,
    local_sems,
    send_sems,
    recv_sems,
):
    nattn, ngrp, nt, width_all = sizes
    rows, width = q_ref.shape
    heads = width // HD
    pool = order_ref.shape[1]
    nzl = nattn // (NX * NCORE)
    nz = nzl * ngrp
    groups = z_groups(nz)
    steps = [0, 1] + list(range(NX - 1, 1, -1))
    chunks = [(dx, 0) for dx in steps] + [(dx, 1) for dx in steps[1:] + [0]]
    index = {chunk: c for c, chunk in enumerate(chunks)}
    nd = nz // 2
    hr = nd * CAP
    nb = nt // 2

    a = lax.axis_index("attn")
    g = lax.axis_index("grp")
    t = lax.axis_index("tp")
    core = lax.rem(a, NCORE)
    zl = lax.rem(a // NCORE, nzl)
    x = a // (NCORE * nzl)
    z = g * nzl + zl

    def at_xz(c, d):
        to = lax.rem(z + d, nz)
        return {
            "attn": (lax.rem(x + c, NX) * nzl + lax.rem(to, nzl)) * NCORE + core,
            "grp": to // nzl,
            "tp": t,
        }

    def at_t(d):
        return {"attn": a, "grp": g, "tp": lax.rem(t + d + nt, nt)}

    sibling = {"attn": a + 1 - 2 * core, "grp": g, "tp": t}

    pairs = [
        (counts_hbm, counts_ref),
        (order_hbm, order_ref),
        (q_hbm, q_ref),
        (nk_hbm, nk_ref),
        (k_hbm, kaug.at[:, :, pl.ds(0, HD)]),
        (v_hbm, vbuf),
        (nv_hbm, nv_ref),
        (res_hbm, res_ref),
        (routes_hbm, routes_ref),
        (rw_hbm, rw_ref),
        (gain_hbm, gain_ref.at[0]),
        (wg_hbm.at[0], wg),
        (wu_hbm.at[0], wu),
        (wd_hbm.at[0], wd),
    ]
    loads = []
    for i, (src, dst) in enumerate(pairs):
        loads.append(pltpu.make_async_copy(src, dst, local_sems.at[i]))
        loads[i].start()

    barrier = pltpu.get_barrier_semaphore()
    partners = [at_t(d) for d in range(1, nt)] + [sibling]
    partners += [at_xz(dx, 0) for dx in range(1, NX)] + [at_xz(0, d) for d in range(1, nz)]
    for partner in partners:
        pl.semaphore_signal(barrier, inc=1, device_id=partner, device_id_type=MESH)

    for i in range(4):
        loads[i].wait()

    sent = []

    def push(src, dst, to):
        index = len(sent)
        copy = pltpu.make_async_remote_copy(
            src_ref=src,
            dst_ref=dst,
            send_sem=send_sems.at[index],
            recv_sem=recv_sems.at[index],
            device_id=to,
            device_id_type=MESH,
        )
        copy.start()
        sent.append(copy)
        return copy

    counts_col = to_column(counts_ref[...].astype(F32), rows)
    starts_row = before(counts_col, HD)
    counts_row = to_row(counts_col, HD)
    place = iota((pool, HD), 0).astype(F32)
    row_of_place = ((place >= starts_row) & (place < starts_row + counts_row)).astype(F32)
    place_of_page = (iota((pool, pool), 0) == order_ref[...]).astype(F32)
    owner = dot(place_of_page.astype(BF16), row_of_place.astype(BF16))
    kaug[:, :, pl.ds(HD, HD)] = jnp.broadcast_to(
        owner.reshape(pool, 1, HD), (pool, PAGE, HD)
    ).astype(BF16)
    own_row = iota((rows, HD), 0)
    lane = iota((rows, HD), 1)
    mask_block = jnp.where((own_row == lane) | (lane >= rows), 0.0, MASKED)

    q_wide = q_ref[...].astype(F32)
    q_rows = jnp.concatenate([q_wide[:, h * HD : (h + 1) * HD] for h in range(heads)], axis=0)
    q_aug = jnp.concatenate(
        [q_rows, jnp.concatenate([mask_block] * heads, axis=0)], axis=1
    ).astype(BF16)
    scale = 1.0 / math.sqrt(HD)
    new_key = jnp.concatenate([nk_ref[...].astype(F32)] * heads, axis=0)
    own = jnp.sum(q_rows * new_key, axis=1, keepdims=True) * scale

    loads[4].wait()
    pieces = scores.shape[0]
    pages = pool // pieces
    tokens = pages * PAGE

    def score_piece(i, top):
        keys = kaug[pl.ds(i * pages, pages)].reshape(tokens, 2 * HD)
        piece = (
            lax.dot_general(
                q_aug, keys, (((1,), (1,)), ((), ())), preferred_element_type=F32
            )
            * scale
        )
        scores[i] = piece
        return jnp.maximum(top, piece)

    top = lax.fori_loop(
        0, pieces, score_piece, jnp.full((heads * rows, tokens), MASKED, F32), unroll=True
    )
    top = jnp.maximum(jnp.max(top, axis=1, keepdims=True), own)
    own_weight = jnp.exp(own - top)

    loads[5].wait()

    def value_piece(i, carry):
        total, mixed = carry
        weights = jnp.exp(scores[i] - top)
        values = vbuf[pl.ds(i * pages, pages)].reshape(tokens, HD)
        return total + weights, mixed + dot(weights.astype(BF16), values)

    total, mixed = lax.fori_loop(
        0,
        pieces,
        value_piece,
        (jnp.zeros((heads * rows, tokens), F32), jnp.zeros((heads * rows, HD), F32)),
        unroll=True,
    )
    total = jnp.sum(total, axis=1, keepdims=True) + own_weight
    for i in range(6, 11):
        loads[i].wait()
    own_low = own_weight.astype(BF16).astype(F32)
    new_value = jnp.concatenate([nv_ref[...].astype(F32)] * heads, axis=0)
    attention = (mixed + own_low * new_value) / total
    attention = jnp.concatenate(
        [attention[h * rows : (h + 1) * rows] for h in range(heads)], axis=1
    )
    hidden = (res_ref[...].astype(F32) + attention).astype(BF16).astype(F32)
    hid[...] = hidden
    routes = routes_ref[...]
    route_weights = rw_ref[...]
    chosen, gated = [], []
    for e in range(ngrp):
        named = routes == e
        hit_row = jnp.max(named.astype(F32), axis=0, keepdims=True)
        gate_row = jnp.sum(jnp.where(named, route_weights, 0.0), axis=0, keepdims=True)
        hit_col = to_column(hit_row, PADR)
        gate_col = to_column(gate_row, PADR)
        pos_row = before(hit_col, PADR)
        pos_col = to_column(pos_row, PADR)
        hit_wide = to_row(hit_col, PADR)
        slot = iota((SLOT, PADR), 0).astype(F32)
        chosen.append(jnp.where(slot == pos_row, hit_wide, 0.0))
        slot = iota((PADR, SLOT), 1).astype(F32)
        gated.append(jnp.where(slot == pos_col, hit_col * gate_col, 0.0))
    chooser = jnp.concatenate(chosen, axis=0).astype(BF16)
    gating = jnp.concatenate(gated, axis=1)

    pl.semaphore_wait(barrier, len(partners))

    padding = jnp.zeros((PADR - rows, width), F32)
    padded_rows = jnp.concatenate([hid[...], padding], axis=0).astype(BF16)
    outgoing = dot(chooser, padded_rows).astype(BF16)
    for e in range(ngrp):
        outg[e] = outgoing[e * SLOT : (e + 1) * SLOT]

    zin_copy, x_copy = {}, {}
    for group in range(2):
        for i, d in enumerate(groups[group]):
            if d:
                expert = lax.rem(z + d, nz) // nzl
                zin_copy[group, i] = push(outg.at[expert], zin.at[group, i], at_xz(0, d))
    zin[0, 0] = outg[g]
    packed = iota((hr, nd * SLOT), 0)
    padded = iota((hr, nd * SLOT), 1)
    match = (packed // CAP == padded // SLOT) & (packed % CAP == padded % SLOT)
    pack = match.astype(F32).astype(BF16)
    gain = gain_ref[...]

    core_copy, rs, sq_copy, ag, home = {}, {}, {}, {}, {}
    seen, squared = set(), set()

    def block(o):
        return lax.rem(t + o + nt, nt)

    def task_in(c):
        dx, group = chunks[c]
        if dx == 0:
            for i, d in enumerate(groups[group]):
                if d:
                    zin_copy[group, i].wait_recv()
            xin[c, 0] = dot(pack, zin[group].reshape(nd * SLOT, width)).astype(BF16)
            core_copy[c] = push(xin.at[c, 0], xin.at[c, 1], sibling)
            for to in steps[1:]:
                far = index[to, group]
                x_copy[far] = push(xin.at[c, 0], xin.at[far, 0], at_xz(to, 0))
        else:
            x_copy[c].wait_recv()
            core_copy[c] = push(xin.at[c, 0], xin.at[c, 1], sibling)

    def task_m1(c):
        core_copy[c].wait_recv()
        slots = xin[c].reshape(2 * hr, width).astype(F32)
        gained = (slots * gain).astype(BF16)
        for part, weight in enumerate((wg, wu)):
            result = dot(gained, weight[...]).astype(BF16)
            for b in range(nb):
                for h in range(2):
                    pre[c, 2 * b + h, part] = result[
                        h * hr : (h + 1) * hr, b * HD : (b + 1) * HD
                    ]
        far = block(4)
        rs[c] = [
            push(pre.at[c, far, 0], rs_half.at[c, 0], at_t(2)),
            push(pre.at[c, far, 1], rs_half.at[c, 1], at_t(-2)),
            push(pre.at[c, block(3)], rs_in.at[c, 0], at_t(1)),
            push(pre.at[c, block(-3)], rs_in.at[c, 1], at_t(-1)),
            push(pre.at[c, block(1)], rs_in.at[c, 2], at_t(1)),
            push(pre.at[c, block(-1)], rs_in.at[c, 3], at_t(-1)),
        ]
        dx, group = chunks[c]
        squares = jnp.sum(slots * slots, axis=1, keepdims=True)
        for h in range(2):
            row = to_row(squares[h * hr : (h + 1) * hr], HD, group * hr)
            sq_own[dx, h] = sq_own[dx, h] + row if dx in seen else row
        if dx in seen:
            sq_copy[dx] = [
                push(sq_own.at[dx, lax.rem(t + d, 2)], sq_in.at[dx, d], at_t(d))
                for d in range(1, nt)
            ]
        seen.add(dx)

    def task_rs2(c):
        out = []
        for way, (here, to) in enumerate(((block(2), at_t(2)), (block(-2), at_t(-2)))):
            rs[c][way].wait_recv()
            rs[c][2 + way].wait_recv()
            near = rs_in[c, way].astype(F32)
            pre[c, here, way] = (
                pre[c, here, way].astype(F32) + near[way] + rs_half[c, way].astype(F32)
            ).astype(BF16)
            other = 1 - way
            pre[c, here, other] = (pre[c, here, other].astype(F32) + near[other]).astype(BF16)
            out.append(push(pre.at[c, here], rs_in.at[c, 4 + way], to))
        rs[c] = rs[c][4:] + out

    def task_silu(c):
        dx, group = chunks[c]
        for copy in rs[c] + ([] if dx in squared else sq_copy[dx]):
            copy.wait_recv()
        squared.add(dx)
        squares = sq_own[dx, lax.rem(t, 2)]
        for d in range(1, nt):
            squares = squares + sq_in[dx, d]
        scale_row = lax.rsqrt(squares / width_all + NORM_EPSILON)
        scale = to_column(scale_row, hr, group * hr)
        total = pre[c, t].astype(F32)
        for i in range(2, 6):
            total = total + rs_in[c, i].astype(F32)
        gate, up = total[0] * scale, total[1] * scale
        act[c, t] = (gate / (1.0 + jnp.exp(-gate)) * up).astype(BF16)
        own = act.at[c, t]
        ag[c] = [push(own, own, at_t(d)) for d in (2, -2, 1, -1)]

    def task_ag2(c):
        out = []
        for way, d in enumerate((2, -2)):
            ag[c][way].wait_recv()
            arrived = act.at[c, block(-d)]
            if way == c % 2:
                out.append(push(arrived, arrived, at_t(d)))
            out.append(push(arrived, arrived, at_t(d // 2)))
        ag[c] = ag[c][2:] + out

    def task_m2(c):
        for copy in ag[c]:
            copy.wait_recv()
        for h in (1, 0):
            units = jnp.concatenate([act[c, 2 * b + h] for b in range(nb)], axis=1)
            outp[c, h] = dot(units, wd[...]).astype(BF16)
            if h == 1:
                core_copy[c] = push(outp.at[c, 1], core_in.at[c], sibling)

    def both_cores(c):
        core_copy[c].wait_recv()
        return outp[c, 0].astype(F32) + core_in[c].astype(F32)

    def task_home(c):
        dx, group = chunks[c]
        xsend[c] = both_cores(c).astype(BF16)
        x_copy[c] = push(xsend.at[c], xback.at[c], at_xz(NX - dx, 0))

    def task_back(group):
        total = both_cores(index[0, group])
        for dx in steps[1:]:
            c = index[dx, group]
            x_copy[c].wait_recv()
            total = total + xback[c].astype(F32)
        spread = lax.dot_general(
            pack, total.astype(BF16), (((0,), (0,)), ((), ())), preferred_element_type=F32
        )
        zsend[group] = spread.astype(BF16).reshape(nd, SLOT, width)
        for i, d in enumerate(groups[group]):
            if d:
                home[group, i] = push(
                    zsend.at[group, i], zback.at[group, i], at_xz(0, nz - d)
                )
            else:
                zback[group, i] = zsend[group, i]

    tasks = (task_in, task_m1, task_rs2, task_silu, task_ag2, task_m2, task_home, task_back)
    for i in range(11, 14):
        loads[i].wait()
    for task, c in ORDER:
        if c < len(chunks) and (task != HOME or chunks[c][0]):
            tasks[task](c)
    for copy in sent[:-nz]:
        copy.wait_send()

    sums = [None] * nz
    for group in range(2):
        for i, d in enumerate(groups[group]):
            if d:
                home[group, i].wait_recv()
            sums[d] = zback[group, i].astype(F32)
    experts = [jnp.zeros((SLOT, width), F32) for e in range(ngrp)]
    for d in range(nz):
        expert = lax.rem(z + d, nz) // nzl
        for e in range(ngrp):
            experts[e] = experts[e] + sums[d] * (expert == e).astype(F32)
    brought = jnp.concatenate(experts, axis=0).astype(BF16)
    gate_high = gating.astype(BF16)
    gate_low = (gating - gate_high.astype(F32)).astype(BF16)
    expert_sum = dot(gate_high, brought) + dot(gate_low, brought)
    out_ref[...] = (hid[...] + expert_sum[0:rows]).astype(BF16)

    for copy in sent[-nz:]:
        copy.wait_send()


def local(
    sizes,
    queries,
    new_keys,
    new_values,
    key_pages,
    value_pages,
    page_order,
    page_counts,
    residual,
    norm_gain,
    routes,
    route_weights,
    w_gate,
    w_up,
    w_down,
):
    nattn, ngrp, nt, width_all = sizes
    rows, width = queries.shape
    heads = width // HD
    pool = key_pages.shape[0]
    units = w_gate.shape[2]
    nzl = nattn // (NX * NCORE)
    nz = nzl * ngrp
    nc, nd = NX * 2, nz // 2
    hr = nd * CAP
    pieces = pool // 16
    copies = 320
    vmem = pl.BlockSpec(memory_space=pltpu.VMEM)
    hbm = pl.BlockSpec(memory_space=pltpu.HBM)
    return pl.pallas_call(
        functools.partial(kernel, sizes),
        out_shape=jax.ShapeDtypeStruct((rows, width), BF16),
        in_specs=[hbm] * 14,
        out_specs=vmem,
        scratch_shapes=[
            pltpu.VMEM((rows, width), BF16),
            pltpu.VMEM((rows, HD), BF16),
            pltpu.VMEM((rows, HD), BF16),
            pltpu.VMEM((1, pool), jnp.int32),
            pltpu.VMEM((1, rows), jnp.int32),
            pltpu.VMEM((rows, width), BF16),
            pltpu.VMEM((1, width), F32),
            pltpu.VMEM((2, rows), jnp.int32),
            pltpu.VMEM((2, rows), F32),
            pltpu.VMEM((pool, PAGE, 2 * HD), BF16),
            pltpu.VMEM((pool, PAGE, HD), BF16),
            pltpu.VMEM((width, units), BF16),
            pltpu.VMEM((width, units), BF16),
            pltpu.VMEM((units, width), BF16),
            pltpu.VMEM((pieces, heads * rows, 16 * PAGE), F32),
            pltpu.VMEM((NX, 2, 1, HD), F32),
            pltpu.VMEM((NX, nt, 1, HD), F32),
            pltpu.VMEM((rows, width), F32),
            pltpu.VMEM((ngrp, SLOT, width), BF16),
            pltpu.VMEM((2, nd, SLOT, width), BF16),
            pltpu.VMEM((nc, 2, hr, width), BF16),
            pltpu.VMEM((nc, nt, 2, hr, HD), BF16),
            pltpu.VMEM((nc, 2, hr, HD), BF16),
            pltpu.VMEM((nc, 6, 2, hr, HD), BF16),
            pltpu.VMEM((nc, nt, hr, HD), BF16),
            pltpu.VMEM((nc, 2, hr, width), BF16),
            pltpu.VMEM((nc, hr, width), BF16),
            pltpu.VMEM((nc, hr, width), BF16),
            pltpu.VMEM((nc, hr, width), BF16),
            pltpu.VMEM((2, nd, SLOT, width), BF16),
            pltpu.VMEM((2, nd, SLOT, width), BF16),
            pltpu.SemaphoreType.DMA((14,)),
            pltpu.SemaphoreType.DMA((copies,)),
            pltpu.SemaphoreType.DMA((copies,)),
        ],
        compiler_params=pltpu.CompilerParams(
            collective_id=0, has_side_effects=True, vmem_limit_bytes=60 * 1024 * 1024
        ),
    )(
        queries,
        new_keys,
        new_values,
        page_order,
        page_counts,
        residual,
        norm_gain,
        routes.T,
        route_weights.T,
        key_pages,
        value_pages,
        w_gate,
        w_up,
        w_down,
    )


def solution(mesh):
    sizes = (mesh.shape["attn"], mesh.shape["grp"], mesh.shape["tp"])

    def whole(*arrays):
        return jax.shard_map(
            functools.partial(local, sizes + (arrays[0].shape[1],)),
            mesh=mesh,
            in_specs=(
                P(("attn", "grp"), "tp"),
                P(("attn", "grp"), "tp"),
                P(("attn", "grp"), "tp"),
                P(("attn", "grp"), None, "tp"),
                P(("attn", "grp"), None, "tp"),
                P(("attn", "grp"), None),
                P(("attn", "grp"), None),
                P(("attn", "grp"), "tp"),
                P("tp"),
                P(("attn", "grp"), None),
                P(("attn", "grp"), None),
                P("grp", "tp", "attn"),
                P("grp", "tp", "attn"),
                P("grp", "attn", "tp"),
            ),
            out_specs=P(("attn", "grp"), "tp"),
            check_vma=False,
        )(*arrays)

    return whole
```

```python
import functools
import math

import jax
import jax.numpy as jnp
from jax import lax
from jax.experimental import pallas as pl
from jax.experimental.pallas import tpu as pltpu
from jax.sharding import PartitionSpec as P

HD = 128
PAGE = 16
CAP = 12
SLOT = 16
PADR = 32
NX = 4
NCORE = 2
NORM_EPSILON = 1e-05
MASKED = -1e30
MESH = pl.DeviceIdType.MESH
IN, M1, RS2, RS3, RS4, SILU, AG2, AG3, AG4, M2, HOME, BACK = range(12)
ORDER = (
    (IN, 0), (M1, 0), (IN, 7), (IN, 1), (IN, 2), (M1, 7), (M1, 2), (M1, 1), (IN, 3), (IN, 4),
    (M1, 3), (IN, 5), (M1, 4), (IN, 6), (M1, 6), (RS2, 2), (M1, 5), (RS2, 3), (RS2, 1),
    (RS2, 4), (RS2, 5), (RS2, 6), (SILU, 2), (SILU, 3), (RS2, 0), (SILU, 1), (SILU, 5),
    (SILU, 6), (RS2, 7), (AG2, 3), (SILU, 4), (AG2, 2), (AG2, 1), (AG2, 5), (AG2, 6),
    (SILU, 0), (SILU, 7), (M2, 3), (AG2, 4), (M2, 2), (HOME, 3), (M2, 1), (HOME, 2), (M2, 5),
    (M2, 6), (AG2, 0), (HOME, 1), (HOME, 5), (AG2, 7), (HOME, 6), (M2, 4), (HOME, 4), (M2, 0),
    (M2, 7), (BACK, 0), (BACK, 1),
)
SUM_BY_ONE = ()
GATHER_BY_ONE = ()
F32 = jnp.float32
BF16 = jnp.bfloat16


def z_groups(nz):
    if nz == 2:
        return ((0,), (1,))
    quarter = nz // 4
    near = tuple(range(quarter + 1)) + tuple(range(nz - quarter + 1, nz))
    return near, tuple(d for d in range(nz) if d not in near)


def iota(shape, dim):
    return lax.broadcasted_iota(jnp.int32, shape, dim)


def to_column(row, rows, start=0):
    n = row.shape[1]
    eye = iota((rows, n), 0) + start == iota((rows, n), 1)
    return jnp.sum(jnp.where(eye, row, jnp.zeros_like(row)), axis=1, keepdims=True)


def to_row(column, lanes, start=0):
    n = column.shape[0]
    eye = iota((n, lanes), 0) + start == iota((n, lanes), 1)
    return jnp.sum(jnp.where(eye, column, jnp.zeros_like(column)), axis=0, keepdims=True)


def before(column, lanes):
    n = column.shape[0]
    ahead = iota((n, lanes), 0) < iota((n, lanes), 1)
    return jnp.sum(jnp.where(ahead, column, jnp.zeros_like(column)), axis=0, keepdims=True)


def dot(a, b):
    return jnp.dot(a, b, preferred_element_type=F32)


def kernel(
    sizes,
    q_hbm,
    nk_hbm,
    nv_hbm,
    order_hbm,
    counts_hbm,
    res_hbm,
    gain_hbm,
    routes_hbm,
    rw_hbm,
    k_hbm,
    v_hbm,
    wg_hbm,
    wu_hbm,
    wd_hbm,
    out_ref,
    q_ref,
    nk_ref,
    nv_ref,
    order_ref,
    counts_ref,
    res_ref,
    gain_ref,
    routes_ref,
    rw_ref,
    kaug,
    vbuf,
    wg,
    wu,
    wd,
    scores,
    sq_own,
    sq_in,
    hid,
    outg,
    zin,
    xin,
    pre,
    rs_half,
    rs_in,
    act,
    outp,
    core_in,
    xsend,
    xback,
    zsend,
    zback,
    local_sems,
    send_sems,
    recv_sems,
):
    nattn, ngrp, nt, width_all = sizes
    rows, width = q_ref.shape
    heads = width // HD
    pool = order_ref.shape[1]
    nzl = nattn // (NX * NCORE)
    nz = nzl * ngrp
    groups = z_groups(nz)
    steps = [0, 1] + list(range(NX - 1, 1, -1))
    chunks = [(dx, 0) for dx in steps] + [(dx, 1) for dx in steps[1:] + [0]]
    index = {chunk: c for c, chunk in enumerate(chunks)}
    nd = nz // 2
    hr = nd * CAP
    nb = nt // 2

    a = lax.axis_index("attn")
    g = lax.axis_index("grp")
    t = lax.axis_index("tp")
    core = lax.rem(a, NCORE)
    zl = lax.rem(a // NCORE, nzl)
    x = a // (NCORE * nzl)
    z = g * nzl + zl

    def at_xz(c, d):
        to = lax.rem(z + d, nz)
        return {
            "attn": (lax.rem(x + c, NX) * nzl + lax.rem(to, nzl)) * NCORE + core,
            "grp": to // nzl,
            "tp": t,
        }

    def at_t(d):
        return {"attn": a, "grp": g, "tp": lax.rem(t + d + nt, nt)}

    sibling = {"attn": a + 1 - 2 * core, "grp": g, "tp": t}

    pairs = [
        (counts_hbm, counts_ref),
        (order_hbm, order_ref),
        (q_hbm, q_ref),
        (nk_hbm, nk_ref),
        (k_hbm, kaug.at[:, :, pl.ds(0, HD)]),
        (v_hbm, vbuf),
        (nv_hbm, nv_ref),
        (res_hbm, res_ref),
        (routes_hbm, routes_ref),
        (rw_hbm, rw_ref),
        (gain_hbm, gain_ref.at[0]),
        (wg_hbm.at[0], wg),
        (wu_hbm.at[0], wu),
        (wd_hbm.at[0], wd),
    ]
    loads = []
    for i, (src, dst) in enumerate(pairs):
        loads.append(pltpu.make_async_copy(src, dst, local_sems.at[i]))
        loads[i].start()

    barrier = pltpu.get_barrier_semaphore()
    partners = [at_t(d) for d in range(1, nt)] + [sibling]
    partners += [at_xz(dx, 0) for dx in range(1, NX)] + [at_xz(0, d) for d in range(1, nz)]
    for partner in partners:
        pl.semaphore_signal(barrier, inc=1, device_id=partner, device_id_type=MESH)

    for i in range(4):
        loads[i].wait()

    sent = []

    def push(src, dst, to):
        index = len(sent)
        copy = pltpu.make_async_remote_copy(
            src_ref=src,
            dst_ref=dst,
            send_sem=send_sems.at[index],
            recv_sem=recv_sems.at[index],
            device_id=to,
            device_id_type=MESH,
        )
        copy.start()
        sent.append(copy)
        return copy

    counts_col = to_column(counts_ref[...].astype(F32), rows)
    starts_row = before(counts_col, HD)
    counts_row = to_row(counts_col, HD)
    place = iota((pool, HD), 0).astype(F32)
    row_of_place = ((place >= starts_row) & (place < starts_row + counts_row)).astype(F32)
    place_of_page = (iota((pool, pool), 0) == order_ref[...]).astype(F32)
    owner = dot(place_of_page.astype(BF16), row_of_place.astype(BF16))
    kaug[:, :, pl.ds(HD, HD)] = jnp.broadcast_to(
        owner.reshape(pool, 1, HD), (pool, PAGE, HD)
    ).astype(BF16)
    own_row = iota((rows, HD), 0)
    lane = iota((rows, HD), 1)
    mask_block = jnp.where((own_row == lane) | (lane >= rows), 0.0, MASKED)

    q_wide = q_ref[...].astype(F32)
    q_rows = jnp.concatenate([q_wide[:, h * HD : (h + 1) * HD] for h in range(heads)], axis=0)
    q_aug = jnp.concatenate(
        [q_rows, jnp.concatenate([mask_block] * heads, axis=0)], axis=1
    ).astype(BF16)
    scale = 1.0 / math.sqrt(HD)
    new_key = jnp.concatenate([nk_ref[...].astype(F32)] * heads, axis=0)
    own = jnp.sum(q_rows * new_key, axis=1, keepdims=True) * scale

    loads[4].wait()
    pieces = scores.shape[0]
    pages = pool // pieces
    tokens = pages * PAGE

    def score_piece(i, top):
        keys = kaug[pl.ds(i * pages, pages)].reshape(tokens, 2 * HD)
        piece = (
            lax.dot_general(
                q_aug, keys, (((1,), (1,)), ((), ())), preferred_element_type=F32
            )
            * scale
        )
        scores[i] = piece
        return jnp.maximum(top, piece)

    top = lax.fori_loop(
        0, pieces, score_piece, jnp.full((heads * rows, tokens), MASKED, F32), unroll=True
    )
    top = jnp.maximum(jnp.max(top, axis=1, keepdims=True), own)
    own_weight = jnp.exp(own - top)

    loads[5].wait()

    def value_piece(i, carry):
        total, mixed = carry
        weights = jnp.exp(scores[i] - top)
        values = vbuf[pl.ds(i * pages, pages)].reshape(tokens, HD)
        return total + weights, mixed + dot(weights.astype(BF16), values)

    total, mixed = lax.fori_loop(
        0,
        pieces,
        value_piece,
        (jnp.zeros((heads * rows, tokens), F32), jnp.zeros((heads * rows, HD), F32)),
        unroll=True,
    )
    total = jnp.sum(total, axis=1, keepdims=True) + own_weight
    for i in range(6, 11):
        loads[i].wait()
    own_low = own_weight.astype(BF16).astype(F32)
    new_value = jnp.concatenate([nv_ref[...].astype(F32)] * heads, axis=0)
    attention = (mixed + own_low * new_value) / total
    attention = jnp.concatenate(
        [attention[h * rows : (h + 1) * rows] for h in range(heads)], axis=1
    )
    hidden = (res_ref[...].astype(F32) + attention).astype(BF16).astype(F32)
    hid[...] = hidden
    routes = routes_ref[...]
    route_weights = rw_ref[...]
    chosen, gated = [], []
    for e in range(ngrp):
        named = routes == e
        hit_row = jnp.max(named.astype(F32), axis=0, keepdims=True)
        gate_row = jnp.sum(jnp.where(named, route_weights, 0.0), axis=0, keepdims=True)
        hit_col = to_column(hit_row, PADR)
        gate_col = to_column(gate_row, PADR)
        pos_row = before(hit_col, PADR)
        pos_col = to_column(pos_row, PADR)
        hit_wide = to_row(hit_col, PADR)
        slot = iota((SLOT, PADR), 0).astype(F32)
        chosen.append(jnp.where(slot == pos_row, hit_wide, 0.0))
        slot = iota((PADR, SLOT), 1).astype(F32)
        gated.append(jnp.where(slot == pos_col, hit_col * gate_col, 0.0))
    chooser = jnp.concatenate(chosen, axis=0).astype(BF16)
    gating = jnp.concatenate(gated, axis=1)

    pl.semaphore_wait(barrier, len(partners))

    padding = jnp.zeros((PADR - rows, width), F32)
    padded_rows = jnp.concatenate([hid[...], padding], axis=0).astype(BF16)
    outgoing = dot(chooser, padded_rows).astype(BF16)
    for e in range(ngrp):
        outg[e] = outgoing[e * SLOT : (e + 1) * SLOT]

    zin_copy, x_copy = {}, {}
    for group in range(2):
        for i, d in enumerate(groups[group]):
            if d:
                expert = lax.rem(z + d, nz) // nzl
                zin_copy[group, i] = push(outg.at[expert], zin.at[group, i], at_xz(0, d))
    zin[0, 0] = outg[g]
    packed = iota((hr, nd * SLOT), 0)
    padded = iota((hr, nd * SLOT), 1)
    match = (packed // CAP == padded // SLOT) & (packed % CAP == padded % SLOT)
    pack = match.astype(F32).astype(BF16)
    gain = gain_ref[...]

    core_copy, rs, sq_copy, ag, home = {}, {}, {}, {}, {}
    seen, squared = set(), set()

    def block(o):
        return lax.rem(t + o + nt, nt)

    def task_in(c):
        dx, group = chunks[c]
        if dx == 0:
            for i, d in enumerate(groups[group]):
                if d:
                    zin_copy[group, i].wait_recv()
            xin[c, 0] = dot(pack, zin[group].reshape(nd * SLOT, width)).astype(BF16)
            core_copy[c] = push(xin.at[c, 0], xin.at[c, 1], sibling)
            for to in steps[1:]:
                far = index[to, group]
                x_copy[far] = push(xin.at[c, 0], xin.at[far, 0], at_xz(to, 0))
        else:
            x_copy[c].wait_recv()
            core_copy[c] = push(xin.at[c, 0], xin.at[c, 1], sibling)

    def task_m1(c):
        core_copy[c].wait_recv()
        slots = xin[c].reshape(2 * hr, width).astype(F32)
        gained = (slots * gain).astype(BF16)
        for part, weight in enumerate((wg, wu)):
            result = dot(gained, weight[...]).astype(BF16)
            for b in range(nb):
                for h in range(2):
                    pre[c, 2 * b + h, part] = result[
                        h * hr : (h + 1) * hr, b * HD : (b + 1) * HD
                    ]
        far = block(4)
        if c in SUM_BY_ONE:
            rs[c] = [
                push(pre.at[c, far, 0], rs_half.at[c, 0], at_t(1)),
                push(pre.at[c, far, 1], rs_half.at[c, 1], at_t(-1)),
            ]
        else:
            rs[c] = [
                push(pre.at[c, far, 0], rs_half.at[c, 0], at_t(2)),
                push(pre.at[c, far, 1], rs_half.at[c, 1], at_t(-2)),
                push(pre.at[c, block(3)], rs_in.at[c, 0], at_t(1)),
                push(pre.at[c, block(-3)], rs_in.at[c, 1], at_t(-1)),
                push(pre.at[c, block(1)], rs_in.at[c, 2], at_t(1)),
                push(pre.at[c, block(-1)], rs_in.at[c, 3], at_t(-1)),
            ]
        dx, group = chunks[c]
        squares = jnp.sum(slots * slots, axis=1, keepdims=True)
        for h in range(2):
            row = to_row(squares[h * hr : (h + 1) * hr], HD, group * hr)
            sq_own[dx, h] = sq_own[dx, h] + row if dx in seen else row
        if dx in seen:
            sq_copy[dx] = [
                push(sq_own.at[dx, lax.rem(t + d, 2)], sq_in.at[dx, d], at_t(d))
                for d in range(1, nt)
            ]
        seen.add(dx)

    def task_rs_by_one(c, step):
        out = []
        for way, (here, to) in enumerate(((4 - step, 1), (step - 4, -1))):
            rs[c][way].wait_recv()
            here = block(here)
            if step == 1:
                pre[c, here, way] = (
                    pre[c, here, way].astype(F32) + rs_half[c, way].astype(F32)
                ).astype(BF16)
            else:
                pre[c, here] = (
                    pre[c, here].astype(F32) + rs_in[c, 3 * way + step - 2].astype(F32)
                ).astype(BF16)
            out.append(push(pre.at[c, here], rs_in.at[c, 3 * way + step - 1], at_t(to)))
        rs[c] = out

    def task_rs3(c):
        task_rs_by_one(c, 2)

    def task_rs4(c):
        task_rs_by_one(c, 3)

    def task_rs2(c):
        if c in SUM_BY_ONE:
            return task_rs_by_one(c, 1)
        out = []
        for way, (here, to) in enumerate(((block(2), at_t(2)), (block(-2), at_t(-2)))):
            rs[c][way].wait_recv()
            rs[c][2 + way].wait_recv()
            near = rs_in[c, way].astype(F32)
            pre[c, here, way] = (
                pre[c, here, way].astype(F32) + near[way] + rs_half[c, way].astype(F32)
            ).astype(BF16)
            other = 1 - way
            pre[c, here, other] = (pre[c, here, other].astype(F32) + near[other]).astype(BF16)
            out.append(push(pre.at[c, here], rs_in.at[c, 4 + way], to))
        rs[c] = rs[c][4:] + out

    def task_silu(c):
        dx, group = chunks[c]
        for copy in rs[c] + ([] if dx in squared else sq_copy[dx]):
            copy.wait_recv()
        squared.add(dx)
        squares = sq_own[dx, lax.rem(t, 2)]
        for d in range(1, nt):
            squares = squares + sq_in[dx, d]
        scale_row = lax.rsqrt(squares / width_all + NORM_EPSILON)
        scale = to_column(scale_row, hr, group * hr)
        total = pre[c, t].astype(F32)
        for i in (2, 5) if c in SUM_BY_ONE else range(2, 6):
            total = total + rs_in[c, i].astype(F32)
        gate, up = total[0] * scale, total[1] * scale
        act[c, t] = (gate / (1.0 + jnp.exp(-gate)) * up).astype(BF16)
        own = act.at[c, t]
        steps_y = (1, -1) if c in GATHER_BY_ONE else (2, -2, 1, -1)
        ag[c] = [push(own, own, at_t(d)) for d in steps_y]

    def task_ag_by_one(c, hop):
        out = []
        for way, d in enumerate((1, -1)):
            ag[c][way].wait_recv()
            if hop < 3 or way == c % 2:
                arrived = act.at[c, block(-d * hop)]
                out.append(push(arrived, arrived, at_t(d)))
        ag[c] = out

    def task_ag3(c):
        task_ag_by_one(c, 2)

    def task_ag4(c):
        task_ag_by_one(c, 3)

    def task_ag2(c):
        if c in GATHER_BY_ONE:
            return task_ag_by_one(c, 1)
        out = []
        for way, d in enumerate((2, -2)):
            ag[c][way].wait_recv()
            arrived = act.at[c, block(-d)]
            if way == c % 2:
                out.append(push(arrived, arrived, at_t(d)))
            out.append(push(arrived, arrived, at_t(d // 2)))
        ag[c] = ag[c][2:] + out

    def task_m2(c):
        for copy in ag[c]:
            copy.wait_recv()
        for h in (1, 0):
            units = jnp.concatenate([act[c, 2 * b + h] for b in range(nb)], axis=1)
            outp[c, h] = dot(units, wd[...]).astype(BF16)
            if h == 1:
                core_copy[c] = push(outp.at[c, 1], core_in.at[c], sibling)

    def both_cores(c):
        core_copy[c].wait_recv()
        return outp[c, 0].astype(F32) + core_in[c].astype(F32)

    def task_home(c):
        dx, group = chunks[c]
        xsend[c] = both_cores(c).astype(BF16)
        x_copy[c] = push(xsend.at[c], xback.at[c], at_xz(NX - dx, 0))

    def task_back(group):
        total = both_cores(index[0, group])
        for dx in steps[1:]:
            c = index[dx, group]
            x_copy[c].wait_recv()
            total = total + xback[c].astype(F32)
        spread = lax.dot_general(
            pack, total.astype(BF16), (((0,), (0,)), ((), ())), preferred_element_type=F32
        )
        zsend[group] = spread.astype(BF16).reshape(nd, SLOT, width)
        for i, d in enumerate(groups[group]):
            if d:
                home[group, i] = push(
                    zsend.at[group, i], zback.at[group, i], at_xz(0, nz - d)
                )
            else:
                zback[group, i] = zsend[group, i]

    tasks = (
        task_in,
        task_m1,
        task_rs2,
        task_rs3,
        task_rs4,
        task_silu,
        task_ag2,
        task_ag3,
        task_ag4,
        task_m2,
        task_home,
        task_back,
    )
    for i in range(11, 14):
        loads[i].wait()
    for task, c in ORDER:
        if c < len(chunks) and (task != HOME or chunks[c][0]):
            tasks[task](c)
    for copy in sent[:-nz]:
        copy.wait_send()

    sums = [None] * nz
    for group in range(2):
        for i, d in enumerate(groups[group]):
            if d:
                home[group, i].wait_recv()
            sums[d] = zback[group, i].astype(F32)
    experts = [jnp.zeros((SLOT, width), F32) for e in range(ngrp)]
    for d in range(nz):
        expert = lax.rem(z + d, nz) // nzl
        for e in range(ngrp):
            experts[e] = experts[e] + sums[d] * (expert == e).astype(F32)
    brought = jnp.concatenate(experts, axis=0).astype(BF16)
    gate_high = gating.astype(BF16)
    gate_low = (gating - gate_high.astype(F32)).astype(BF16)
    expert_sum = dot(gate_high, brought) + dot(gate_low, brought)
    out_ref[...] = (hid[...] + expert_sum[0:rows]).astype(BF16)

    for copy in sent[-nz:]:
        copy.wait_send()


def local(
    sizes,
    queries,
    new_keys,
    new_values,
    key_pages,
    value_pages,
    page_order,
    page_counts,
    residual,
    norm_gain,
    routes,
    route_weights,
    w_gate,
    w_up,
    w_down,
):
    nattn, ngrp, nt, width_all = sizes
    rows, width = queries.shape
    heads = width // HD
    pool = key_pages.shape[0]
    units = w_gate.shape[2]
    nzl = nattn // (NX * NCORE)
    nz = nzl * ngrp
    nc, nd = NX * 2, nz // 2
    hr = nd * CAP
    pieces = pool // 16
    copies = 320
    vmem = pl.BlockSpec(memory_space=pltpu.VMEM)
    hbm = pl.BlockSpec(memory_space=pltpu.HBM)
    return pl.pallas_call(
        functools.partial(kernel, sizes),
        out_shape=jax.ShapeDtypeStruct((rows, width), BF16),
        in_specs=[hbm] * 14,
        out_specs=vmem,
        scratch_shapes=[
            pltpu.VMEM((rows, width), BF16),
            pltpu.VMEM((rows, HD), BF16),
            pltpu.VMEM((rows, HD), BF16),
            pltpu.VMEM((1, pool), jnp.int32),
            pltpu.VMEM((1, rows), jnp.int32),
            pltpu.VMEM((rows, width), BF16),
            pltpu.VMEM((1, width), F32),
            pltpu.VMEM((2, rows), jnp.int32),
            pltpu.VMEM((2, rows), F32),
            pltpu.VMEM((pool, PAGE, 2 * HD), BF16),
            pltpu.VMEM((pool, PAGE, HD), BF16),
            pltpu.VMEM((width, units), BF16),
            pltpu.VMEM((width, units), BF16),
            pltpu.VMEM((units, width), BF16),
            pltpu.VMEM((pieces, heads * rows, 16 * PAGE), F32),
            pltpu.VMEM((NX, 2, 1, HD), F32),
            pltpu.VMEM((NX, nt, 1, HD), F32),
            pltpu.VMEM((rows, width), F32),
            pltpu.VMEM((ngrp, SLOT, width), BF16),
            pltpu.VMEM((2, nd, SLOT, width), BF16),
            pltpu.VMEM((nc, 2, hr, width), BF16),
            pltpu.VMEM((nc, nt, 2, hr, HD), BF16),
            pltpu.VMEM((nc, 2, hr, HD), BF16),
            pltpu.VMEM((nc, 6, 2, hr, HD), BF16),
            pltpu.VMEM((nc, nt, hr, HD), BF16),
            pltpu.VMEM((nc, 2, hr, width), BF16),
            pltpu.VMEM((nc, hr, width), BF16),
            pltpu.VMEM((nc, hr, width), BF16),
            pltpu.VMEM((nc, hr, width), BF16),
            pltpu.VMEM((2, nd, SLOT, width), BF16),
            pltpu.VMEM((2, nd, SLOT, width), BF16),
            pltpu.SemaphoreType.DMA((14,)),
            pltpu.SemaphoreType.DMA((copies,)),
            pltpu.SemaphoreType.DMA((copies,)),
        ],
        compiler_params=pltpu.CompilerParams(
            collective_id=0, has_side_effects=True, vmem_limit_bytes=60 * 1024 * 1024
        ),
    )(
        queries,
        new_keys,
        new_values,
        page_order,
        page_counts,
        residual,
        norm_gain,
        routes.T,
        route_weights.T,
        key_pages,
        value_pages,
        w_gate,
        w_up,
        w_down,
    )


def solution(mesh):
    sizes = (mesh.shape["attn"], mesh.shape["grp"], mesh.shape["tp"])

    def whole(*arrays):
        return jax.shard_map(
            functools.partial(local, sizes + (arrays[0].shape[1],)),
            mesh=mesh,
            in_specs=(
                P(("attn", "grp"), "tp"),
                P(("attn", "grp"), "tp"),
                P(("attn", "grp"), "tp"),
                P(("attn", "grp"), None, "tp"),
                P(("attn", "grp"), None, "tp"),
                P(("attn", "grp"), None),
                P(("attn", "grp"), None),
                P(("attn", "grp"), "tp"),
                P("tp"),
                P(("attn", "grp"), None),
                P(("attn", "grp"), None),
                P("grp", "tp", "attn"),
                P("grp", "tp", "attn"),
                P("grp", "attn", "tp"),
            ),
            out_specs=P(("attn", "grp"), "tp"),
            check_vma=False,
        )(*arrays)

    return whole
```

```python
import functools
import math

import jax
import jax.numpy as jnp
from jax import lax
from jax.experimental import pallas as pl
from jax.experimental.pallas import tpu as pltpu
from jax.sharding import PartitionSpec as P

HD = 128
PAGE = 16
CAP = 12
SLOT = 16
PADR = 32
NX = 4
NCORE = 2
NORM_EPSILON = 1e-05
MASKED = -1e30
MESH = pl.DeviceIdType.MESH
IN, M1, RS2, RS3, RS4, SILU, AG2, AG3, AG4, M2, HOME, BACK = range(12)
ORDER = (
    (IN, 0), (M1, 0), (IN, 7), (IN, 1), (IN, 2), (M1, 7), (M1, 2), (M1, 1), (IN, 3), (IN, 4),
    (M1, 3), (IN, 5), (M1, 4), (IN, 6), (M1, 6), (RS2, 2), (M1, 5), (RS2, 3), (RS2, 1),
    (RS2, 4), (RS2, 5), (RS2, 6), (SILU, 2), (SILU, 3), (RS2, 0), (SILU, 1), (SILU, 5),
    (SILU, 6), (RS2, 7), (AG2, 3), (SILU, 4), (AG2, 2), (AG2, 1), (AG2, 5), (AG2, 6),
    (SILU, 0), (SILU, 7), (M2, 3), (AG2, 4), (M2, 2), (HOME, 3), (M2, 1), (HOME, 2), (M2, 5),
    (M2, 6), (AG2, 0), (HOME, 1), (HOME, 5), (AG2, 7), (HOME, 6), (M2, 4), (HOME, 4), (M2, 0),
    (M2, 7), (BACK, 0), (BACK, 1),
)
SUM_BY_ONE = ()
GATHER_BY_ONE = ()
F32 = jnp.float32
BF16 = jnp.bfloat16


def z_groups(nz):
    if nz == 2:
        return ((0,), (1,))
    quarter = nz // 4
    near = tuple(range(quarter + 1)) + tuple(range(nz - quarter + 1, nz))
    return near, tuple(d for d in range(nz) if d not in near)


def iota(shape, dim):
    return lax.broadcasted_iota(jnp.int32, shape, dim)


def to_column(row, rows, start=0):
    n = row.shape[1]
    eye = iota((rows, n), 0) + start == iota((rows, n), 1)
    return jnp.sum(jnp.where(eye, row, jnp.zeros_like(row)), axis=1, keepdims=True)


def to_row(column, lanes, start=0):
    n = column.shape[0]
    eye = iota((n, lanes), 0) + start == iota((n, lanes), 1)
    return jnp.sum(jnp.where(eye, column, jnp.zeros_like(column)), axis=0, keepdims=True)


def before(column, lanes):
    n = column.shape[0]
    ahead = iota((n, lanes), 0) < iota((n, lanes), 1)
    return jnp.sum(jnp.where(ahead, column, jnp.zeros_like(column)), axis=0, keepdims=True)


def dot(a, b):
    return jnp.dot(a, b, preferred_element_type=F32)


def kernel(
    sizes,
    q_hbm,
    nk_hbm,
    nv_hbm,
    order_hbm,
    counts_hbm,
    res_hbm,
    gain_hbm,
    routes_hbm,
    rw_hbm,
    k_hbm,
    v_hbm,
    wg_hbm,
    wu_hbm,
    wd_hbm,
    out_ref,
    q_ref,
    nk_ref,
    nv_ref,
    order_ref,
    counts_ref,
    res_ref,
    gain_ref,
    routes_ref,
    rw_ref,
    kaug,
    vbuf,
    wg,
    wu,
    wd,
    scores,
    sq_own,
    sq_in,
    hid,
    outg,
    zin,
    xin,
    pre,
    rs_half,
    rs_in,
    act,
    outp,
    core_in,
    xsend,
    xback,
    zsend,
    zback,
    local_sems,
    send_sems,
    recv_sems,
):
    nattn, ngrp, nt, width_all = sizes
    rows, width = q_ref.shape
    heads = width // HD
    pool = order_ref.shape[1]
    nzl = nattn // (NX * NCORE)
    nz = nzl * ngrp
    groups = z_groups(nz)
    steps = [0, 1] + list(range(NX - 1, 1, -1))
    chunks = [(dx, 0) for dx in steps] + [(dx, 1) for dx in steps[1:] + [0]]
    index = {chunk: c for c, chunk in enumerate(chunks)}
    nd = nz // 2
    hr = nd * CAP
    nb = nt // 2

    a = lax.axis_index("attn")
    g = lax.axis_index("grp")
    t = lax.axis_index("tp")
    core = lax.rem(a, NCORE)
    zl = lax.rem(a // NCORE, nzl)
    x = a // (NCORE * nzl)
    z = g * nzl + zl

    def at_xz(c, d):
        to = lax.rem(z + d, nz)
        return {
            "attn": (lax.rem(x + c, NX) * nzl + lax.rem(to, nzl)) * NCORE + core,
            "grp": to // nzl,
            "tp": t,
        }

    def at_t(d):
        return {"attn": a, "grp": g, "tp": lax.rem(t + d + nt, nt)}

    sibling = {"attn": a + 1 - 2 * core, "grp": g, "tp": t}

    pairs = [
        (counts_hbm, counts_ref),
        (order_hbm, order_ref),
        (q_hbm, q_ref),
        (nk_hbm, nk_ref),
        (k_hbm, kaug.at[:, :, pl.ds(0, HD)]),
        (v_hbm, vbuf),
        (nv_hbm, nv_ref),
        (res_hbm, res_ref),
        (routes_hbm, routes_ref),
        (rw_hbm, rw_ref),
        (gain_hbm, gain_ref.at[0]),
        (wg_hbm.at[0], wg),
        (wu_hbm.at[0], wu),
        (wd_hbm.at[0], wd),
    ]
    loads = []
    for i, (src, dst) in enumerate(pairs):
        loads.append(pltpu.make_async_copy(src, dst, local_sems.at[i]))
        if i < 11:
            loads[i].start()

    barrier = pltpu.get_barrier_semaphore()
    partners = [at_t(d) for d in range(1, nt)] + [sibling]
    partners += [at_xz(dx, 0) for dx in range(1, NX)] + [at_xz(0, d) for d in range(1, nz)]
    for partner in partners:
        pl.semaphore_signal(barrier, inc=1, device_id=partner, device_id_type=MESH)

    for i in range(4):
        loads[i].wait()

    sent = []

    def push(src, dst, to):
        index = len(sent)
        copy = pltpu.make_async_remote_copy(
            src_ref=src,
            dst_ref=dst,
            send_sem=send_sems.at[index],
            recv_sem=recv_sems.at[index],
            device_id=to,
            device_id_type=MESH,
        )
        copy.start()
        sent.append(copy)
        return copy

    counts_col = to_column(counts_ref[...].astype(F32), rows)
    starts_row = before(counts_col, HD)
    counts_row = to_row(counts_col, HD)
    place = iota((pool, HD), 0).astype(F32)
    row_of_place = ((place >= starts_row) & (place < starts_row + counts_row)).astype(F32)
    place_of_page = (iota((pool, pool), 0) == order_ref[...]).astype(F32)
    owner = dot(place_of_page.astype(BF16), row_of_place.astype(BF16))
    kaug[:, :, pl.ds(HD, HD)] = jnp.broadcast_to(
        owner.reshape(pool, 1, HD), (pool, PAGE, HD)
    ).astype(BF16)
    own_row = iota((rows, HD), 0)
    lane = iota((rows, HD), 1)
    mask_block = jnp.where((own_row == lane) | (lane >= rows), 0.0, MASKED)

    q_wide = q_ref[...].astype(F32)
    q_rows = jnp.concatenate([q_wide[:, h * HD : (h + 1) * HD] for h in range(heads)], axis=0)
    q_aug = jnp.concatenate(
        [q_rows, jnp.concatenate([mask_block] * heads, axis=0)], axis=1
    ).astype(BF16)
    scale = 1.0 / math.sqrt(HD)
    new_key = jnp.concatenate([nk_ref[...].astype(F32)] * heads, axis=0)
    own = jnp.sum(q_rows * new_key, axis=1, keepdims=True) * scale

    loads[4].wait()
    for i in range(11, 14):
        loads[i].start()
    pieces = scores.shape[0]
    pages = pool // pieces
    tokens = pages * PAGE

    def score_piece(i, top):
        keys = kaug[pl.ds(i * pages, pages)].reshape(tokens, 2 * HD)
        piece = (
            lax.dot_general(
                q_aug, keys, (((1,), (1,)), ((), ())), preferred_element_type=F32
            )
            * scale
        )
        scores[i] = piece
        return jnp.maximum(top, piece)

    top = lax.fori_loop(
        0, pieces, score_piece, jnp.full((heads * rows, tokens), MASKED, F32), unroll=True
    )
    top = jnp.maximum(jnp.max(top, axis=1, keepdims=True), own)
    own_weight = jnp.exp(own - top)

    loads[5].wait()

    def value_piece(i, carry):
        total, mixed = carry
        weights = jnp.exp(scores[i] - top)
        values = vbuf[pl.ds(i * pages, pages)].reshape(tokens, HD)
        return total + weights, mixed + dot(weights.astype(BF16), values)

    total, mixed = lax.fori_loop(
        0,
        pieces,
        value_piece,
        (jnp.zeros((heads * rows, tokens), F32), jnp.zeros((heads * rows, HD), F32)),
        unroll=True,
    )
    total = jnp.sum(total, axis=1, keepdims=True) + own_weight
    for i in range(6, 11):
        loads[i].wait()
    own_low = own_weight.astype(BF16).astype(F32)
    new_value = jnp.concatenate([nv_ref[...].astype(F32)] * heads, axis=0)
    attention = (mixed + own_low * new_value) / total
    attention = jnp.concatenate(
        [attention[h * rows : (h + 1) * rows] for h in range(heads)], axis=1
    )
    hidden = (res_ref[...].astype(F32) + attention).astype(BF16).astype(F32)
    hid[...] = hidden
    routes = routes_ref[...]
    route_weights = rw_ref[...]
    chosen, gated = [], []
    for e in range(ngrp):
        named = routes == e
        hit_row = jnp.max(named.astype(F32), axis=0, keepdims=True)
        gate_row = jnp.sum(jnp.where(named, route_weights, 0.0), axis=0, keepdims=True)
        hit_col = to_column(hit_row, PADR)
        gate_col = to_column(gate_row, PADR)
        pos_row = before(hit_col, PADR)
        pos_col = to_column(pos_row, PADR)
        hit_wide = to_row(hit_col, PADR)
        slot = iota((SLOT, PADR), 0).astype(F32)
        chosen.append(jnp.where(slot == pos_row, hit_wide, 0.0))
        slot = iota((PADR, SLOT), 1).astype(F32)
        gated.append(jnp.where(slot == pos_col, hit_col * gate_col, 0.0))
    chooser = jnp.concatenate(chosen, axis=0).astype(BF16)
    gating = jnp.concatenate(gated, axis=1)

    pl.semaphore_wait(barrier, len(partners))

    padding = jnp.zeros((PADR - rows, width), F32)
    padded_rows = jnp.concatenate([hid[...], padding], axis=0).astype(BF16)
    outgoing = dot(chooser, padded_rows).astype(BF16)
    for e in range(ngrp):
        outg[e] = outgoing[e * SLOT : (e + 1) * SLOT]

    zin_copy, x_copy = {}, {}
    for group in range(2):
        for i, d in enumerate(groups[group]):
            if d:
                expert = lax.rem(z + d, nz) // nzl
                zin_copy[group, i] = push(outg.at[expert], zin.at[group, i], at_xz(0, d))
    zin[0, 0] = outg[g]
    packed = iota((hr, nd * SLOT), 0)
    padded = iota((hr, nd * SLOT), 1)
    match = (packed // CAP == padded // SLOT) & (packed % CAP == padded % SLOT)
    pack = match.astype(F32).astype(BF16)
    gain = gain_ref[...]

    core_copy, rs, sq_copy, ag, home = {}, {}, {}, {}, {}
    seen, squared = set(), set()

    def block(o):
        return lax.rem(t + o + nt, nt)

    def task_in(c):
        dx, group = chunks[c]
        if dx == 0:
            for i, d in enumerate(groups[group]):
                if d:
                    zin_copy[group, i].wait_recv()
            xin[c, 0] = dot(pack, zin[group].reshape(nd * SLOT, width)).astype(BF16)
            core_copy[c] = push(xin.at[c, 0], xin.at[c, 1], sibling)
            for to in steps[1:]:
                far = index[to, group]
                x_copy[far] = push(xin.at[c, 0], xin.at[far, 0], at_xz(to, 0))
        else:
            x_copy[c].wait_recv()
            core_copy[c] = push(xin.at[c, 0], xin.at[c, 1], sibling)

    def task_m1(c):
        core_copy[c].wait_recv()
        slots = xin[c].reshape(2 * hr, width).astype(F32)
        gained = (slots * gain).astype(BF16)
        for part, weight in enumerate((wg, wu)):
            result = dot(gained, weight[...]).astype(BF16)
            for b in range(nb):
                for h in range(2):
                    pre[c, 2 * b + h, part] = result[
                        h * hr : (h + 1) * hr, b * HD : (b + 1) * HD
                    ]
        far = block(4)
        if c in SUM_BY_ONE:
            rs[c] = [
                push(pre.at[c, far, 0], rs_half.at[c, 0], at_t(1)),
                push(pre.at[c, far, 1], rs_half.at[c, 1], at_t(-1)),
            ]
        else:
            rs[c] = [
                push(pre.at[c, far, 0], rs_half.at[c, 0], at_t(2)),
                push(pre.at[c, far, 1], rs_half.at[c, 1], at_t(-2)),
                push(pre.at[c, block(3)], rs_in.at[c, 0], at_t(1)),
                push(pre.at[c, block(-3)], rs_in.at[c, 1], at_t(-1)),
                push(pre.at[c, block(1)], rs_in.at[c, 2], at_t(1)),
                push(pre.at[c, block(-1)], rs_in.at[c, 3], at_t(-1)),
            ]
        dx, group = chunks[c]
        squares = jnp.sum(slots * slots, axis=1, keepdims=True)
        for h in range(2):
            row = to_row(squares[h * hr : (h + 1) * hr], HD, group * hr)
            sq_own[dx, h] = sq_own[dx, h] + row if dx in seen else row
        if dx in seen:
            sq_copy[dx] = [
                push(sq_own.at[dx, lax.rem(t + d, 2)], sq_in.at[dx, d], at_t(d))
                for d in range(1, nt)
            ]
        seen.add(dx)

    def task_rs_by_one(c, step):
        out = []
        for way, (here, to) in enumerate(((4 - step, 1), (step - 4, -1))):
            rs[c][way].wait_recv()
            here = block(here)
            if step == 1:
                pre[c, here, way] = (
                    pre[c, here, way].astype(F32) + rs_half[c, way].astype(F32)
                ).astype(BF16)
            else:
                pre[c, here] = (
                    pre[c, here].astype(F32) + rs_in[c, 3 * way + step - 2].astype(F32)
                ).astype(BF16)
            out.append(push(pre.at[c, here], rs_in.at[c, 3 * way + step - 1], at_t(to)))
        rs[c] = out

    def task_rs3(c):
        task_rs_by_one(c, 2)

    def task_rs4(c):
        task_rs_by_one(c, 3)

    def task_rs2(c):
        if c in SUM_BY_ONE:
            return task_rs_by_one(c, 1)
        out = []
        for way, (here, to) in enumerate(((block(2), at_t(2)), (block(-2), at_t(-2)))):
            rs[c][way].wait_recv()
            rs[c][2 + way].wait_recv()
            near = rs_in[c, way].astype(F32)
            pre[c, here, way] = (
                pre[c, here, way].astype(F32) + near[way] + rs_half[c, way].astype(F32)
            ).astype(BF16)
            other = 1 - way
            pre[c, here, other] = (pre[c, here, other].astype(F32) + near[other]).astype(BF16)
            out.append(push(pre.at[c, here], rs_in.at[c, 4 + way], to))
        rs[c] = rs[c][4:] + out

    def task_silu(c):
        dx, group = chunks[c]
        for copy in rs[c] + ([] if dx in squared else sq_copy[dx]):
            copy.wait_recv()
        squared.add(dx)
        squares = sq_own[dx, lax.rem(t, 2)]
        for d in range(1, nt):
            squares = squares + sq_in[dx, d]
        scale_row = lax.rsqrt(squares / width_all + NORM_EPSILON)
        scale = to_column(scale_row, hr, group * hr)
        total = pre[c, t].astype(F32)
        for i in (2, 5) if c in SUM_BY_ONE else range(2, 6):
            total = total + rs_in[c, i].astype(F32)
        gate, up = total[0] * scale, total[1] * scale
        act[c, t] = (gate / (1.0 + jnp.exp(-gate)) * up).astype(BF16)
        own = act.at[c, t]
        steps_y = (1, -1) if c in GATHER_BY_ONE else (2, -2, 1, -1)
        ag[c] = [push(own, own, at_t(d)) for d in steps_y]

    def task_ag_by_one(c, hop):
        out = []
        for way, d in enumerate((1, -1)):
            ag[c][way].wait_recv()
            if hop < 3 or way == c % 2:
                arrived = act.at[c, block(-d * hop)]
                out.append(push(arrived, arrived, at_t(d)))
        ag[c] = out

    def task_ag3(c):
        task_ag_by_one(c, 2)

    def task_ag4(c):
        task_ag_by_one(c, 3)

    def task_ag2(c):
        if c in GATHER_BY_ONE:
            return task_ag_by_one(c, 1)
        out = []
        for way, d in enumerate((2, -2)):
            ag[c][way].wait_recv()
            arrived = act.at[c, block(-d)]
            if way == c % 2:
                out.append(push(arrived, arrived, at_t(d)))
            out.append(push(arrived, arrived, at_t(d // 2)))
        ag[c] = ag[c][2:] + out

    def task_m2(c):
        for copy in ag[c]:
            copy.wait_recv()
        for h in (1, 0):
            units = jnp.concatenate([act[c, 2 * b + h] for b in range(nb)], axis=1)
            outp[c, h] = dot(units, wd[...]).astype(BF16)
            if h == 1:
                core_copy[c] = push(outp.at[c, 1], core_in.at[c], sibling)

    def both_cores(c):
        core_copy[c].wait_recv()
        return outp[c, 0].astype(F32) + core_in[c].astype(F32)

    def task_home(c):
        dx, group = chunks[c]
        xsend[c] = both_cores(c).astype(BF16)
        x_copy[c] = push(xsend.at[c], xback.at[c], at_xz(NX - dx, 0))

    def task_back(group):
        total = both_cores(index[0, group])
        for dx in steps[1:]:
            c = index[dx, group]
            x_copy[c].wait_recv()
            total = total + xback[c].astype(F32)
        padding = jnp.zeros((SLOT - CAP, width), F32)
        for i in range(nd):
            piece = [total[i * CAP : (i + 1) * CAP], padding]
            zsend[group, i] = jnp.concatenate(piece, axis=0).astype(BF16)
        for i, d in enumerate(groups[group]):
            if d:
                home[group, i] = push(
                    zsend.at[group, i], zback.at[group, i], at_xz(0, nz - d)
                )
            else:
                zback[group, i] = zsend[group, i]

    tasks = (
        task_in,
        task_m1,
        task_rs2,
        task_rs3,
        task_rs4,
        task_silu,
        task_ag2,
        task_ag3,
        task_ag4,
        task_m2,
        task_home,
        task_back,
    )
    for i in range(11, 14):
        loads[i].wait()
    for task, c in ORDER:
        if c < len(chunks) and (task != HOME or chunks[c][0]):
            tasks[task](c)
    for copy in sent[:-nz]:
        copy.wait_send()

    sums = [None] * nz
    for group in range(2):
        for i, d in enumerate(groups[group]):
            if d:
                home[group, i].wait_recv()
            sums[d] = zback[group, i].astype(F32)
    experts = [jnp.zeros((SLOT, width), F32) for e in range(ngrp)]
    for d in range(nz):
        expert = lax.rem(z + d, nz) // nzl
        for e in range(ngrp):
            experts[e] = experts[e] + sums[d] * (expert == e).astype(F32)
    brought = jnp.concatenate(experts, axis=0).astype(BF16)
    gate_high = gating.astype(BF16)
    gate_low = (gating - gate_high.astype(F32)).astype(BF16)
    expert_sum = dot(gate_high, brought) + dot(gate_low, brought)
    out_ref[...] = (hid[...] + expert_sum[0:rows]).astype(BF16)

    for copy in sent[-nz:]:
        copy.wait_send()


def local(
    sizes,
    queries,
    new_keys,
    new_values,
    key_pages,
    value_pages,
    page_order,
    page_counts,
    residual,
    norm_gain,
    routes,
    route_weights,
    w_gate,
    w_up,
    w_down,
):
    nattn, ngrp, nt, width_all = sizes
    rows, width = queries.shape
    heads = width // HD
    pool = key_pages.shape[0]
    units = w_gate.shape[2]
    nzl = nattn // (NX * NCORE)
    nz = nzl * ngrp
    nc, nd = NX * 2, nz // 2
    hr = nd * CAP
    pieces = pool // 16
    copies = 320
    vmem = pl.BlockSpec(memory_space=pltpu.VMEM)
    hbm = pl.BlockSpec(memory_space=pltpu.HBM)
    return pl.pallas_call(
        functools.partial(kernel, sizes),
        out_shape=jax.ShapeDtypeStruct((rows, width), BF16),
        in_specs=[hbm] * 14,
        out_specs=vmem,
        scratch_shapes=[
            pltpu.VMEM((rows, width), BF16),
            pltpu.VMEM((rows, HD), BF16),
            pltpu.VMEM((rows, HD), BF16),
            pltpu.VMEM((1, pool), jnp.int32),
            pltpu.VMEM((1, rows), jnp.int32),
            pltpu.VMEM((rows, width), BF16),
            pltpu.VMEM((1, width), F32),
            pltpu.VMEM((2, rows), jnp.int32),
            pltpu.VMEM((2, rows), F32),
            pltpu.VMEM((pool, PAGE, 2 * HD), BF16),
            pltpu.VMEM((pool, PAGE, HD), BF16),
            pltpu.VMEM((width, units), BF16),
            pltpu.VMEM((width, units), BF16),
            pltpu.VMEM((units, width), BF16),
            pltpu.VMEM((pieces, heads * rows, 16 * PAGE), F32),
            pltpu.VMEM((NX, 2, 1, HD), F32),
            pltpu.VMEM((NX, nt, 1, HD), F32),
            pltpu.VMEM((rows, width), F32),
            pltpu.VMEM((ngrp, SLOT, width), BF16),
            pltpu.VMEM((2, nd, SLOT, width), BF16),
            pltpu.VMEM((nc, 2, hr, width), BF16),
            pltpu.VMEM((nc, nt, 2, hr, HD), BF16),
            pltpu.VMEM((nc, 2, hr, HD), BF16),
            pltpu.VMEM((nc, 6, 2, hr, HD), BF16),
            pltpu.VMEM((nc, nt, hr, HD), BF16),
            pltpu.VMEM((nc, 2, hr, width), BF16),
            pltpu.VMEM((nc, hr, width), BF16),
            pltpu.VMEM((nc, hr, width), BF16),
            pltpu.VMEM((nc, hr, width), BF16),
            pltpu.VMEM((2, nd, SLOT, width), BF16),
            pltpu.VMEM((2, nd, SLOT, width), BF16),
            pltpu.SemaphoreType.DMA((14,)),
            pltpu.SemaphoreType.DMA((copies,)),
            pltpu.SemaphoreType.DMA((copies,)),
        ],
        compiler_params=pltpu.CompilerParams(
            collective_id=0, has_side_effects=True, vmem_limit_bytes=60 * 1024 * 1024
        ),
    )(
        queries,
        new_keys,
        new_values,
        page_order,
        page_counts,
        residual,
        norm_gain,
        routes.T,
        route_weights.T,
        key_pages,
        value_pages,
        w_gate,
        w_up,
        w_down,
    )


def solution(mesh):
    sizes = (mesh.shape["attn"], mesh.shape["grp"], mesh.shape["tp"])

    def whole(*arrays):
        return jax.shard_map(
            functools.partial(local, sizes + (arrays[0].shape[1],)),
            mesh=mesh,
            in_specs=(
                P(("attn", "grp"), "tp"),
                P(("attn", "grp"), "tp"),
                P(("attn", "grp"), "tp"),
                P(("attn", "grp"), None, "tp"),
                P(("attn", "grp"), None, "tp"),
                P(("attn", "grp"), None),
                P(("attn", "grp"), None),
                P(("attn", "grp"), "tp"),
                P("tp"),
                P(("attn", "grp"), None),
                P(("attn", "grp"), None),
                P("grp", "tp", "attn"),
                P("grp", "tp", "attn"),
                P("grp", "attn", "tp"),
            ),
            out_specs=P(("attn", "grp"), "tp"),
            check_vma=False,
        )(*arrays)

    return whole
```
